32 devices in a mesh: user: 4 (over y, x), item: 8 (over z, core).
Axes of the slice: x: 2, y: 2, z: 4, core: 2. Of those that a mesh axis runs over, the one named last changes fastest.
Arguments:
- item_features: bfloat16 [1024, 256], P('item'), may hold values from -6 to 6
- level_weights: bfloat16 [3, 256, 512], replicated, may hold values from -0.21875 to 0.21875
- tile_values: bfloat16 [4, 8, 24, 128, 128], P('user', 'item'), may hold values from -0.1875 to 0.1875
- tile_order: int32 [4, 96], P('user'), may hold values from 0 to 95, each once within a row
- tile_counts: int32 [4, 8], P('user'), may hold values from 1 to 24, 96 in all within a row
- cotangent: bfloat16 [2048, 512], P(('user', 'item')), may hold values from -6 to 6
Outputs:
- hidden: bfloat16 [2048, 512], P(('user', 'item'))
- item_grad: float32 [1024, 256], P('item')
- weight_grad: float32 [3, 256, 512], replicated
The draws below stay inside these ranges and needn't reach their ends.
Inputs may be any that keep to these rules, and one draw needn't show every extreme that they name: `tile_order`: each row is a permutation of all 96 slots of the group. `tile_counts`: each row sums to 96; in every row some cell holds exactly 24 tiles.
All inputs are finite; a program needn't handle non-finite values.
Results may differ from the reference program's by a relative error of at most 0.009.
Values may be sent and summed in bfloat16 or wider, within the bound.
No kernel may reach another device: no remote copies, remote signals or barrier semaphores. Data moves between devices by JAX's collectives and lax.ppermute only.
A program may use at most 64 MiB of HBM per device.

```python
import math
import jax
import jax.numpy as jnp
import numpy as np
from jax import lax

D = 256
H = 512
LEVELS = 3
TILE = 128
UBLK = 4
ITEM_BLK = 1
ITEMS = 1024
USERS = 2048
SLOTS = 96
CAP = 24
N_USER = 4
N_ITEM = 8


def levels(key, dims, cuts, least, high):
    def one(axis_at, parts):
        draws = jax.random.uniform(jax.random.fold_in(jax.random.fold_in(key, 6), axis_at), (parts,), jnp.float32, least / len(cuts), high / len(cuts))
        return jnp.repeat(jnp.exp(draws), dims[axis_at] // parts).reshape((-1,) + (1,) * (len(dims) - axis_at - 1))

    level = one(*cuts[0])
    for cut in cuts[1:]:
        level = level * one(*cut)
    return level


def length_profile(amount, total, reach, skew):
    weights = [(1 << 20) // math.isqrt(rank ** skew) + 1 for rank in range(2, amount + 1)]
    surplus, holding = total - reach - (amount - 1), [1] * (amount - 1)
    while surplus > 0:
        candidates = [i for i in range(amount - 1) if holding[i] < reach]
        mass, budget = sum([weights[i] for i in candidates]), surplus
        for i in candidates:
            extra = min(reach - holding[i], max(1, budget * weights[i] // mass), surplus)
            holding[i] = holding[i] + extra
            surplus = surplus - extra
    return np.array([reach] + holding)


def uneven(key, number_of, total, most, skew):
    if number_of == 2:
        one = jax.random.randint(key, (), max(1, total - most), min(most, total - 1) + 1)
        return jnp.stack([one, total - one])
    tallies = jnp.asarray(length_profile(number_of, total, most, skew), jnp.int32)
    pairs = (number_of - 1) // 2
    donor, sink = tallies[1:1 + 2 * pairs:2], tallies[2:2 + 2 * pairs:2]
    room = jnp.minimum(donor - 1, most - sink)
    passed = jax.random.randint(jax.random.fold_in(key, 1), (pairs,), 0, 1 << 20) % (room + 1)
    tallies = tallies.at[1:1 + 2 * pairs:2].set(donor - passed).at[2:2 + 2 * pairs:2].set(sink + passed)
    return tallies[jax.random.permutation(jax.random.fold_in(key, 2), number_of)]


def normal_values(key, dims, width, bound, cuts=(), dtype=jnp.bfloat16):
    factor_of = levels(key, dims, cuts, -0.22, 0.18) if cuts else 1.0
    array = jax.random.normal(key, dims, jnp.float32) * width * factor_of
    return jnp.minimum(jnp.maximum(array, -bound), bound).astype(dtype)


def setup_inputs(seed: int = 0) -> dict:
    keys = jax.random.split(jax.random.key(seed), 7)
    item_features = normal_values(keys[0], (ITEMS, D), 1.0, 6.0, ((0, 8),))
    level_weights = normal_values(keys[1], (LEVELS, D, H), (LEVELS * D) ** -0.5, 0.21875)
    tile_values = normal_values(keys[2], (N_USER, N_ITEM, CAP, TILE, TILE), ITEMS ** -0.5, 0.1875, ((0, 4), (1, 8)))
    tile_order = jax.vmap(lambda own: jax.random.permutation(own, SLOTS))(jax.random.split(keys[3], N_USER)).reshape((N_USER, SLOTS)).astype(jnp.int32)
    tile_counts = jax.vmap(lambda own: uneven(own, N_ITEM, SLOTS, CAP, 2))(jax.random.split(keys[4], N_USER)).reshape((N_USER, N_ITEM)).astype(jnp.int32)
    cotangent = normal_values(keys[5], (USERS, H), 1.0, 6.0, ((0, 32),))
    return {"item_features": item_features, "level_weights": level_weights, "tile_values": tile_values, "tile_order": tile_order, "tile_counts": tile_counts, "cotangent": cotangent}


def silu_slope(values):
    sigmoid_v = jax.nn.sigmoid(values)
    return sigmoid_v * (1.0 + values * (1.0 - sigmoid_v))

def reference(item_features, level_weights, tile_values, tile_order, tile_counts, cotangent):
    block_count = ITEM_BLK * N_ITEM
    group_rows = UBLK * TILE
    weights_wide = level_weights.astype(jnp.float32)
    cot_groups = cotangent.reshape(N_USER, group_rows, H)

    def cell_lists(order_row, count_row):
        before = (jnp.cumsum(count_row) - count_row).astype(jnp.int32)
        padded = jnp.concatenate([order_row.astype(jnp.int32), jnp.zeros((CAP,), jnp.int32)])
        slot_ids = jax.vmap(lambda offset: lax.dynamic_slice(padded, (offset,), (CAP,)))(before)
        live_slots = jnp.arange(CAP)[None, :] < count_row[:, None]
        return (slot_ids, live_slots)

    def decode(slot_id):
        level_of = slot_id // (UBLK * block_count)
        user_block = slot_id // block_count % UBLK
        item_block = slot_id % block_count
        return (level_of, user_block, item_block)

    def group_pass(inputs):
        tiles_group, order_row, count_row, cot_rows = inputs
        slot_ids, live_slots = cell_lists(order_row, count_row)

        def cell_forward(tiles_cell, slots_cell, live_cell):

            def advance(running, position):
                level_of, user_block, item_block = decode(slots_cell[position])
                features = lax.dynamic_slice_in_dim(item_features, (item_block * TILE).astype(jnp.int32), TILE, 0)
                product = jnp.dot(tiles_cell[position], features, preferred_element_type=jnp.float32)
                product = product * live_cell[position].astype(jnp.float32)
                first_row = ((level_of * UBLK + user_block) * TILE).astype(jnp.int32)
                current = lax.dynamic_slice_in_dim(running, first_row, TILE, 0)
                return (lax.dynamic_update_slice_in_dim(running, current + product, first_row, 0), None)
            start_value = jnp.zeros((LEVELS * group_rows, D), jnp.float32)
            running, unused = lax.scan(advance, start_value, jnp.arange(CAP))
            return running.astype(jnp.bfloat16)
        aggregates = jax.vmap(cell_forward)(tiles_group, slot_ids, live_slots)
        summed = lax.optimization_barrier(jnp.sum(aggregates.astype(jnp.float32), axis=0)).reshape(LEVELS, group_rows, D)
        pre_act = jnp.einsum('rud,rdh->uh', summed, weights_wide, precision=lax.Precision.HIGHEST)
        hidden = jax.nn.silu(pre_act).astype(jnp.bfloat16)
        slope_rows = (cot_rows.astype(jnp.float32) * silu_slope(pre_act)).astype(jnp.bfloat16)
        slope_wide = slope_rows.astype(jnp.float32)
        grad_terms = jnp.einsum('rud,uh->rdh', summed, slope_wide, precision=lax.Precision.HIGHEST)
        back_rows = jnp.einsum('uh,rdh->rud', slope_wide, weights_wide, precision=lax.Precision.HIGHEST)
        back_rows = back_rows.astype(jnp.bfloat16).reshape(LEVELS * group_rows, D)

        def cell_backward(tiles_cell, slots_cell, live_cell):

            def advance(running, position):
                level_of, user_block, item_block = decode(slots_cell[position])
                first_row = ((level_of * UBLK + user_block) * TILE).astype(jnp.int32)
                rows_back = lax.dynamic_slice_in_dim(back_rows, first_row, TILE, 0)
                product = jnp.dot(tiles_cell[position].T, rows_back, preferred_element_type=jnp.float32)
                product = product * live_cell[position].astype(jnp.float32)
                item_row = (item_block * TILE).astype(jnp.int32)
                current = lax.dynamic_slice_in_dim(running, item_row, TILE, 0)
                return (lax.dynamic_update_slice_in_dim(running, current + product, item_row, 0), None)
            start_value = jnp.zeros((block_count * TILE, D), jnp.float32)
            running, unused = lax.scan(advance, start_value, jnp.arange(CAP))
            return running
        item_parts = jax.vmap(cell_backward)(tiles_group, slot_ids, live_slots)
        item_total = lax.optimization_barrier(jnp.sum(item_parts, axis=0))
        return (hidden, grad_terms, item_total)
    outputs = lax.map(group_pass, (tile_values, tile_order, tile_counts, cot_groups))
    hidden_all = outputs[0].reshape(USERS, H)
    weight_grad = lax.optimization_barrier(jnp.sum(outputs[1], axis=0)) / jnp.sqrt(jnp.float32(USERS))
    item_grad = lax.optimization_barrier(jnp.sum(outputs[2], axis=0))
    return (hidden_all, item_grad, weight_grad)
```

```python
import functools
import jax
import jax.numpy as jnp
from jax import lax
from jax.experimental import pallas as pl
from jax.experimental.pallas import tpu as pltpu
from jax.sharding import PartitionSpec as P

BF16 = jnp.bfloat16
F32 = jnp.float32
VMEM_LIMIT = 24 * 1024 * 1024


def partners(axis, step):
    return [(i, i ^ step) for i in range(lax.axis_size(axis))]


def swap(array, axis, step):
    return lax.ppermute(array, axis, partners(axis, step))


def tree_sum(parts):
    while len(parts) > 1:
        parts = [parts[i] + parts[i + 1] for i in range(0, len(parts), 2)]
    return parts[0]


def call(body, out_shapes, args, scratch=(), specs=None, cost=None):
    vmem = pl.BlockSpec(memory_space=pltpu.VMEM)
    return pl.pallas_call(
        body,
        out_shape=out_shapes,
        in_specs=specs if specs is not None else [vmem] * len(args),
        out_specs=jax.tree.map(lambda _: vmem, out_shapes),
        scratch_shapes=list(scratch),
        compiler_params=pltpu.CompilerParams(vmem_limit_bytes=VMEM_LIMIT),
        cost_estimate=cost,
    )(*args)


def struct(shape, dtype):
    return jax.ShapeDtypeStruct(shape, dtype)


def place_tiles(block_count, order, counts, tiles, dense, sems):
    tile = tiles.shape[-1]
    capacity = tiles.shape[2]
    cell = lax.axis_index("item")
    before = jnp.int32(0)
    for c in range(counts.shape[1]):
        before = before + jnp.where(c < cell, counts[0, c], 0)
    holding = counts[0, cell]
    dense[...] = jnp.zeros_like(dense)

    def copy(t):
        slot = order[0, jnp.minimum(before + t, order.shape[1] - 1)]
        row = pl.multiple_of((slot // block_count) * tile, tile)
        column = pl.multiple_of((slot % block_count) * tile, tile)
        return pltpu.make_async_copy(
            tiles.at[0, 0, t], dense.at[pl.ds(row, tile), pl.ds(column, tile)], sems.at[t]
        )

    for t in range(capacity):
        @pl.when(t < holding)
        def _():
            copy(t).start()
    for t in range(capacity):
        @pl.when(t < holding)
        def _():
            copy(t).wait()


def forward(chips, dense, weights, *refs):
    pieces = refs[: 2 * chips]
    aggregate, keep, send, features = refs[2 * chips:]
    core = lax.axis_index("item") % 2
    chip = lax.axis_index("item") // 2
    levels, width, hidden = weights.shape
    tile = pieces[0].shape[0]
    for k in range(chips):
        for other in range(2):
            block = 2 * (chip ^ k) + (core ^ other)
            features[pl.ds(pl.multiple_of(block * tile, tile), tile), :] = pieces[2 * k + other][...]
    group_rows = dense.shape[0] // levels
    share = keep.shape[1]
    step = min(256, group_rows)
    for first in range(0, group_rows, step):
        total = jnp.zeros((step, hidden), F32)
        for r in range(levels):
            rows = pl.ds(r * group_rows + first, step)
            block = jnp.dot(dense[rows, :], features[...], preferred_element_type=F32).astype(BF16)
            aggregate[rows, :] = block
            total = total + jnp.dot(block, weights[r], preferred_element_type=F32)
        for at in range(0, step, 2 * share):
            z = (first + at) // (2 * share)
            even = total[at:at + share]
            odd = total[at + share:at + 2 * share]
            keep[z] = jnp.where(core == 0, even, odd)
            send[z] = jnp.where(core == 0, odd, even).astype(BF16)


def pair_sum(chips, keep, got, own, *sends):
    chip = lax.axis_index("item") // 2
    own[...] = (keep[chip].astype(F32) + got[chip].astype(F32)).astype(own.dtype)
    for k in range(1, chips):
        sends[k - 1][...] = (keep[chip ^ k].astype(F32) + got[chip ^ k].astype(F32)).astype(BF16)


def activate(own, *refs):
    *parts, cotangent, hidden, slope = refs
    pre = own[...]
    for part in parts:
        pre = pre + part[...].astype(F32)
    sigmoid = 1.0 / (1.0 + jnp.exp(-pre))
    hidden[...] = (pre * sigmoid).astype(BF16)
    slope[...] = (cotangent[...].astype(F32) * (sigmoid * (1.0 + pre * (1.0 - sigmoid)))).astype(BF16)


def gather_slopes(chips, pieces, slopes):
    core = lax.axis_index("item") % 2
    chip = lax.axis_index("item") // 2
    share = pieces[0].shape[0]
    for k in range(chips):
        for other in range(2):
            block = 2 * (chip ^ k) + (core ^ other)
            slopes[pl.ds(pl.multiple_of(block * share, share), share), :] = pieces[2 * k + other][...]


def backward(chips, dense, weights, *refs):
    pieces = refs[: 2 * chips]
    slopes, keep, send, back = refs[2 * chips:]
    gather_slopes(chips, pieces, slopes)
    core = lax.axis_index("item") % 2
    levels, width, hidden = weights.shape
    group_rows = slopes.shape[0]
    for r in range(levels):
        back[pl.ds(r * group_rows, group_rows), :] = lax.dot_general(
            slopes[...], weights[r], (((1,), (1,)), ((), ())), preferred_element_type=F32
        ).astype(BF16)
    tile = keep.shape[1]
    for z in range(keep.shape[0]):
        both = lax.dot_general(
            dense[:, pl.ds(2 * z * tile, 2 * tile)], back[...],
            (((0,), (0,)), ((), ())), preferred_element_type=F32,
        )
        even, odd = both[:tile], both[tile:]
        keep[z] = jnp.where(core == 0, even, odd)
        send[z] = jnp.where(core == 0, odd, even).astype(BF16)


def weight_terms(aggregate, slopes, keep, send):
    core = lax.axis_index("item") % 2
    levels = keep.shape[1]
    group_rows = slopes.shape[0]
    half = aggregate.shape[1] // 2
    chips = keep.shape[0]
    part = half // chips
    for r in range(levels):
        both = lax.dot_general(
            aggregate[pl.ds(r * group_rows, group_rows), :], slopes[...],
            (((0,), (0,)), ((), ())), preferred_element_type=F32,
        )
        low, high = both[:half], both[half:]
        mine = jnp.where(core == 0, low, high)
        theirs = jnp.where(core == 0, high, low).astype(BF16)
        for z in range(chips):
            keep[z, r] = mine[z * part:(z + 1) * part]
            send[z, r] = theirs[z * part:(z + 1) * part]


def round_sum(*refs):
    *parts, out = refs
    total = parts[0][...].astype(F32)
    for part in parts[1:]:
        total = total + part[...].astype(F32)
    out[...] = total.astype(out.dtype)


def tree_round(*refs):
    *parts, out = refs
    out[...] = tree_sum([part[...].astype(F32) for part in parts]).astype(out.dtype)


def assemble(chips, scale, *refs):
    *pieces, out = refs
    core = lax.axis_index("item") % 2
    chip = lax.axis_index("item") // 2
    levels, part, hidden = pieces[0].shape
    half = out.shape[1] // 2
    for k in range(chips):
        for other in range(2):
            row = (core ^ other) * half + (chip ^ k) * part
            out[:, pl.ds(pl.multiple_of(row, part), part), :] = pieces[2 * k + other][...].astype(F32) * scale


def per_device(item_features, level_weights, tile_values, tile_order, tile_counts, cotangent):
    item_size = lax.axis_size("item")
    user_size = lax.axis_size("user")
    chips = item_size // 2
    levels, width, hidden_width = level_weights.shape
    tile = tile_values.shape[-1]
    capacity = tile_values.shape[2]
    local_items = item_features.shape[0]
    items = local_items * item_size
    block_count = items // tile
    user_blocks = tile_order.shape[1] // (levels * block_count)
    group_rows = user_blocks * tile
    share = group_rows // item_size
    vmem = pl.BlockSpec(memory_space=pltpu.VMEM)
    smem = pl.BlockSpec(memory_space=pltpu.SMEM)

    pieces = [item_features] + [swap(item_features, "item", 2 * k) for k in range(1, chips)]
    feature_pieces = []
    for piece in pieces:
        feature_pieces += [piece, swap(piece, "item", 1)]

    dense = call(
        functools.partial(place_tiles, block_count),
        struct((levels * group_rows, items), BF16),
        (tile_order, tile_counts, tile_values),
        scratch=[pltpu.SemaphoreType.DMA((capacity,))],
        specs=[smem, smem, pl.BlockSpec(memory_space=pl.ANY)],
    )
    aggregate, pre_keep, pre_send = call(
        functools.partial(forward, chips),
        (
            struct((levels * group_rows, width), BF16),
            struct((chips, share, hidden_width), F32),
            struct((chips, share, hidden_width), BF16),
        ),
        (dense, level_weights, *feature_pieces),
        scratch=[pltpu.VMEM((items, width), BF16)],
    )
    pre_got = swap(pre_send, "item", 1)
    pre_own, *pre_sends = call(
        functools.partial(pair_sum, chips),
        (struct((share, hidden_width), F32),) + (struct((share, hidden_width), BF16),) * (chips - 1),
        (pre_keep, pre_got),
    )
    pre_parts = [swap(pre_sends[k - 1], "item", 2 * k) for k in range(1, chips)]
    hidden, slope = call(
        activate,
        (struct((share, hidden_width), BF16),) * 2,
        (pre_own, *pre_parts, cotangent),
    )
    pieces = [slope] + [swap(slope, "item", 2 * k) for k in range(1, chips)]
    slope_pieces = []
    for piece in pieces:
        slope_pieces += [piece, swap(piece, "item", 1)]

    slopes, item_keep, item_send = call(
        functools.partial(backward, chips),
        (
            struct((group_rows, hidden_width), BF16),
            struct((chips, tile, width), F32),
            struct((chips, tile, width), BF16),
        ),
        (dense, level_weights, *slope_pieces),
        scratch=[pltpu.VMEM((levels * group_rows, width), BF16)],
    )
    item_got = swap(item_send, "item", 1)
    part = width // item_size
    grad_keep, grad_send = call(
        weight_terms,
        (
            struct((chips, levels, part, hidden_width), F32),
            struct((chips, levels, part, hidden_width), BF16),
        ),
        (aggregate, slopes),
    )
    item_own, *item_sends = call(
        functools.partial(pair_sum, chips),
        (struct((tile, width), F32),) + (struct((tile, width), BF16),) * (chips - 1),
        (item_keep, item_got),
    )
    item_parts = [swap(item_sends[k - 1], "item", 2 * k) for k in range(1, chips)]
    item_group = call(round_sum, struct((tile, width), BF16), (item_own, *item_parts))
    item_all = [item_group] + [swap(item_group, "user", k) for k in range(1, user_size)]
    item_grad = call(tree_round, struct((tile, width), F32), item_all)

    grad_got = swap(grad_send, "item", 1)
    grad_own, *grad_sends = call(
        functools.partial(pair_sum, chips),
        (struct((levels, part, hidden_width), F32),)
        + (struct((levels, part, hidden_width), BF16),) * (chips - 1),
        (grad_keep, grad_got),
    )
    grad_parts = [swap(grad_sends[k - 1], "item", 2 * k) for k in range(1, chips)]
    grad_group = call(round_sum, struct((levels, part, hidden_width), BF16), (grad_own, *grad_parts))
    grad_all = [grad_group] + [swap(grad_group, "user", k) for k in range(1, user_size)]
    grad_piece = call(tree_round, struct((levels, part, hidden_width), BF16), grad_all)
    pieces = [grad_piece] + [swap(grad_piece, "item", 2 * k) for k in range(1, chips)]
    grad_pieces = []
    for piece in pieces:
        grad_pieces += [piece, swap(piece, "item", 1)]
    weight_grad = call(
        functools.partial(assemble, chips, (group_rows * user_size) ** -0.5),
        struct((levels, width, hidden_width), F32),
        grad_pieces,
    )
    return hidden, item_grad, weight_grad


def solution(mesh):
    in_specs = (
        P("item", None),
        P(),
        P("user", "item", None, None, None),
        P("user", None),
        P("user", None),
        P(("user", "item"), None),
    )
    out_specs = (P(("user", "item"), None), P("item", None), P())
    return jax.shard_map(
        per_device, mesh=mesh, in_specs=in_specs, out_specs=out_specs, check_vma=False
    )
```

```python
import functools
import jax
import jax.numpy as jnp
from jax import lax
from jax.experimental import pallas as pl
from jax.experimental.pallas import tpu as pltpu
from jax.sharding import PartitionSpec as P

BF16 = jnp.bfloat16
F32 = jnp.float32
VMEM_LIMIT = 24 * 1024 * 1024


def partners(axis, step):
    return [(i, i ^ step) for i in range(lax.axis_size(axis))]


def swap(array, axis, step):
    return lax.ppermute(array, axis, partners(axis, step))


def tree_sum(parts):
    while len(parts) > 1:
        parts = [parts[i] + parts[i + 1] for i in range(0, len(parts), 2)]
    return parts[0]


def call(body, out_shapes, args, scratch=(), specs=None, cost=None):
    vmem = pl.BlockSpec(memory_space=pltpu.VMEM)
    return pl.pallas_call(
        body,
        out_shape=out_shapes,
        in_specs=specs if specs is not None else [vmem] * len(args),
        out_specs=jax.tree.map(lambda _: vmem, out_shapes),
        scratch_shapes=list(scratch),
        compiler_params=pltpu.CompilerParams(vmem_limit_bytes=VMEM_LIMIT),
        cost_estimate=cost,
    )(*args)


def cost(microseconds):
    return pl.CostEstimate(
        flops=int(microseconds * 1e9), bytes_accessed=int(microseconds * 3e6), transcendentals=0
    )


def struct(shape, dtype):
    return jax.ShapeDtypeStruct(shape, dtype)


def place_tiles(block_count, order, counts, tiles, dense, sems):
    tile = tiles.shape[-1]
    capacity = tiles.shape[2]
    cell = lax.axis_index("item")
    before = jnp.int32(0)
    for c in range(counts.shape[1]):
        before = before + jnp.where(c < cell, counts[0, c], 0)
    holding = counts[0, cell]
    dense[...] = jnp.zeros_like(dense)

    def copy(t):
        slot = order[0, jnp.minimum(before + t, order.shape[1] - 1)]
        row = pl.multiple_of((slot // block_count) * tile, tile)
        column = pl.multiple_of((slot % block_count) * tile, tile)
        return pltpu.make_async_copy(
            tiles.at[0, 0, t], dense.at[pl.ds(row, tile), pl.ds(column, tile)], sems.at[t]
        )

    for t in range(capacity):
        @pl.when(t < holding)
        def _():
            copy(t).start()
    for t in range(capacity):
        @pl.when(t < holding)
        def _():
            copy(t).wait()


def forward(chips, dense, weights, *refs):
    pieces = refs[: 2 * chips]
    aggregate, keep, send, features = refs[2 * chips:]
    core = lax.axis_index("item") % 2
    chip = lax.axis_index("item") // 2
    levels, width, hidden = weights.shape
    tile = pieces[0].shape[0]
    for k in range(chips):
        for other in range(2):
            block = 2 * (chip ^ k) + (core ^ other)
            features[pl.ds(pl.multiple_of(block * tile, tile), tile), :] = pieces[2 * k + other][...]
    group_rows = dense.shape[0] // levels
    share = keep.shape[1]
    step = min(256, group_rows)
    for first in range(0, group_rows, step):
        total = jnp.zeros((step, hidden), F32)
        for r in range(levels):
            rows = pl.ds(r * group_rows + first, step)
            block = jnp.dot(dense[rows, :], features[...], preferred_element_type=F32).astype(BF16)
            aggregate[rows, :] = block
            total = total + jnp.dot(block, weights[r], preferred_element_type=F32)
        for at in range(0, step, 2 * share):
            z = (first + at) // (2 * share)
            even = total[at:at + share]
            odd = total[at + share:at + 2 * share]
            keep[z] = jnp.where(core == 0, even, odd)
            send[z] = jnp.where(core == 0, odd, even).astype(BF16)


def pair_sum(chips, keep, got, own, *sends):
    chip = lax.axis_index("item") // 2
    own[...] = (keep[chip].astype(F32) + got[chip].astype(F32)).astype(own.dtype)
    for k in range(1, chips):
        sends[k - 1][...] = (keep[chip ^ k].astype(F32) + got[chip ^ k].astype(F32)).astype(BF16)


def halve(keep, got, own, send):
    chip = lax.axis_index("item") // 2
    for k in range(0, keep.shape[0], 2):
        own[k // 2] = keep[chip ^ k].astype(F32) + got[chip ^ k].astype(F32)
        k += 1
        send[k // 2] = (keep[chip ^ k].astype(F32) + got[chip ^ k].astype(F32)).astype(BF16)


def activate(own, *refs):
    *parts, cotangent, hidden, slope = refs
    pre = own[...]
    for part in parts:
        pre = pre + part[...].astype(F32)
    sigmoid = 1.0 / (1.0 + jnp.exp(-pre))
    hidden[...] = (pre * sigmoid).astype(BF16)
    slope[...] = (cotangent[...].astype(F32) * (sigmoid * (1.0 + pre * (1.0 - sigmoid)))).astype(BF16)


def gather_slopes(chips, pieces, slopes):
    core = lax.axis_index("item") % 2
    chip = lax.axis_index("item") // 2
    share = pieces[0].shape[0]
    for k in range(chips):
        for other in range(2):
            block = 2 * (chip ^ k) + (core ^ other)
            slopes[pl.ds(pl.multiple_of(block * share, share), share), :] = pieces[2 * k + other][...]


def backward(chips, dense, weights, *refs):
    pieces = refs[: 2 * chips]
    slopes, keep, send, back = refs[2 * chips:]
    gather_slopes(chips, pieces, slopes)
    core = lax.axis_index("item") % 2
    levels, width, hidden = weights.shape
    group_rows = slopes.shape[0]
    for r in range(levels):
        back[pl.ds(r * group_rows, group_rows), :] = lax.dot_general(
            slopes[...], weights[r], (((1,), (1,)), ((), ())), preferred_element_type=F32
        ).astype(BF16)
    users, chips_, few, _ = keep.shape
    tile = users * few
    for z in range(chips_):
        both = lax.dot_general(
            dense[:, pl.ds(2 * z * tile, 2 * tile)], back[...],
            (((0,), (0,)), ((), ())), preferred_element_type=F32,
        )
        even, odd = both[:tile], both[tile:]
        mine = jnp.where(core == 0, even, odd)
        theirs = jnp.where(core == 0, odd, even).astype(BF16)
        for u in range(users):
            keep[u, z] = mine[u * few:(u + 1) * few]
            send[u, z] = theirs[u * few:(u + 1) * few]


def transpose_terms(levels, aggregate, keep, send):
    core = lax.axis_index("item") % 2
    chips, part, _ = keep.shape
    half = chips * part
    step = keep.shape[2] // levels
    for r in range(levels):
        columns = pl.ds(r * step, step)
        turned = aggregate[columns, :].T
        low, high = turned[:half], turned[half:]
        mine = jnp.where(core == 0, low, high)
        theirs = jnp.where(core == 0, high, low)
        for z in range(chips):
            keep[z, :, columns] = mine[z * part:(z + 1) * part]
            send[z, :, columns] = theirs[z * part:(z + 1) * part]


def weight_rows(slopes, keep, got, out, turned):
    group_rows = slopes.shape[0]
    kept, part, columns = keep.shape
    levels = columns // group_rows
    for k in range(kept):
        total = (keep[k] + got[k].astype(F32)).astype(BF16)
        for r in range(levels):
            at = (k * levels + r) * part
            turned[at:at + part, :] = total[:, r * group_rows:(r + 1) * group_rows]
    rows = jnp.dot(turned[...], slopes[...], preferred_element_type=F32)
    users, _, few, lanes = out.shape
    groups = part // few
    for u in range(users):
        for block in range(kept * levels):
            first = block * part + (u % groups) * few
            column = (u // groups) * lanes
            out[u, block] = rows[first:first + few, column:column + lanes]


def user_pieces(keep, got, rows, *outs):
    user = lax.axis_index("user")
    _, chips, few, width = keep.shape
    _, levels, part, lanes = rows.shape
    for k, out in enumerate(outs):
        items = keep[user ^ k] + got[user ^ k].astype(F32)
        at = 0
        for column in range(0, width, lanes):
            for z in range(chips):
                out[at:at + few] = items[z, :, column:column + lanes].astype(out.dtype)
                at += few
        for r in range(levels):
            out[at:at + part] = rows[user ^ k, r].astype(out.dtype)
            at += part
        if at < out.shape[0]:
            out[at:] = jnp.zeros((out.shape[0] - at, lanes), out.dtype)


def chip_pieces(chips, few, blocks, rows, *refs):
    count = len(refs) - chips - 1
    parts, outs, total = refs[:count], refs[count:-1], refs[-1]
    chip = lax.axis_index("item") // 2
    summed = parts[0][...]
    for part in parts[1:]:
        summed = summed + part[...].astype(F32)
    for block in range(blocks):
        for z in range(chips):
            at = (block * chips + z) * few
            total[z, block * few:(block + 1) * few] = summed[at:at + few]
    first = blocks * chips * few
    weight = summed[first:first + rows].astype(BF16)
    for k, out in enumerate(outs):
        out[:blocks * few] = total[chip ^ k].astype(out.dtype)
        out[blocks * few:blocks * few + rows] = weight.astype(out.dtype)
        if blocks * few + rows < out.shape[0]:
            out[blocks * few + rows:] = jnp.zeros((out.shape[0] - blocks * few - rows, out.shape[1]), out.dtype)


def user_rows(items, rows, *refs):
    *parts, out = refs
    total = parts[0][:items]
    for part in parts[1:]:
        total = total + part[:items].astype(F32)
    out[:items] = total.astype(BF16)
    for k in range(len(parts)):
        terms = []
        for j in range(k % 2, len(parts), 2):
            at = items + ((j ^ k) // 2) * rows
            terms.append(parts[j][at:at + rows].astype(BF16).astype(F32))
        out[items + k * rows:items + (k + 1) * rows] = tree_sum(terms).astype(BF16)
    if items + len(parts) * rows < out.shape[0]:
        out[items + len(parts) * rows:] = jnp.zeros((out.shape[0] - items - len(parts) * rows, out.shape[1]), BF16)


def item_rows(few, *refs):
    *parts, out = refs
    user = lax.axis_index("user")
    lanes = parts[0].shape[1]
    for k, part in enumerate(parts):
        row = pl.multiple_of((user ^ k) * few, few)
        for block in range(out.shape[1] // lanes):
            out[pl.ds(row, few), block * lanes:(block + 1) * lanes] = part[block * few:(block + 1) * few].astype(F32)


def weight_out(chips, items, few, scale, *refs):
    *pieces, out, wide = refs
    core = lax.axis_index("item") % 2
    chip = lax.axis_index("item") // 2
    user = lax.axis_index("user")
    levels, width, _ = out.shape
    lanes = pieces[0].shape[1]
    users = len(pieces) // 2
    part = width // (2 * chips)
    groups = part // few
    for other in range(2):
        for j in range(users):
            piece = pieces[users * other + j]
            for k in range(chips):
                at = items + k * levels * few
                for r in range(levels):
                    block = piece[at + r * few:at + (r + 1) * few].astype(F32) * scale
                    if groups == 1 and few % 8 == 0:
                        row = (core ^ other) * (width // 2) + (chip ^ k) * part
                        column = (user ^ j) * lanes
                        out[r, pl.ds(pl.multiple_of(row, few), few),
                            pl.ds(pl.multiple_of(column, lanes), lanes)] = block
                    else:
                        wide[core ^ other, chip ^ k, user ^ j, r] = block
    if not (groups == 1 and few % 8 == 0):
        for c in range(2):
            for z in range(chips):
                for u in range(users):
                    row = c * (width // 2) + z * part + (u % groups) * few
                    column = (u // groups) * lanes
                    for r in range(levels):
                        out[r, row:row + few, column:column + lanes] = wide[c, z, u, r]


def per_device(item_features, level_weights, tile_values, tile_order, tile_counts, cotangent):
    item_size = lax.axis_size("item")
    user_size = lax.axis_size("user")
    chips = item_size // 2
    levels, width, hidden_width = level_weights.shape
    tile = tile_values.shape[-1]
    capacity = tile_values.shape[2]
    local_items = item_features.shape[0]
    items = local_items * item_size
    block_count = items // tile
    user_blocks = tile_order.shape[1] // (levels * block_count)
    group_rows = user_blocks * tile
    share = group_rows // item_size
    vmem = pl.BlockSpec(memory_space=pltpu.VMEM)
    smem = pl.BlockSpec(memory_space=pltpu.SMEM)

    far = [swap(item_features, "item", 2 * k) for k in range(chips - 1, 0, -1)][::-1]
    dense = call(
        functools.partial(place_tiles, block_count),
        struct((levels * group_rows, items), BF16),
        (tile_order, tile_counts, tile_values),
        scratch=[pltpu.SemaphoreType.DMA((capacity,))],
        specs=[smem, smem, pl.BlockSpec(memory_space=pl.ANY)],
        cost=cost(4),
    )
    *far, dense = lax.optimization_barrier((*far, dense))
    feature_pieces = []
    for piece in [item_features, *far]:
        feature_pieces += [piece, swap(piece, "item", 1)]

    aggregate, pre_keep, pre_send = call(
        functools.partial(forward, chips),
        (
            struct((levels * group_rows, width), BF16),
            struct((chips, share, hidden_width), F32),
            struct((chips, share, hidden_width), BF16),
        ),
        (dense, level_weights, *feature_pieces),
        scratch=[pltpu.VMEM((items, width), BF16)],
        cost=cost(2),
    )
    pre_got = swap(pre_send, "item", 1)
    pre_own, *pre_sends = call(
        functools.partial(pair_sum, chips),
        (struct((share, hidden_width), F32),) + (struct((share, hidden_width), BF16),) * (chips - 1),
        (pre_keep, pre_got),
        cost=cost(0.1),
    )
    aggregate, *pre_sends = lax.optimization_barrier((aggregate, *pre_sends))
    pre_parts = [swap(pre_sends[k - 1], "item", 2 * k) for k in range(chips - 1, 0, -1)][::-1]

    part = width // item_size
    turned = struct((chips, part, levels * group_rows), BF16)

    turned_keep, turned_send = call(
        functools.partial(transpose_terms, levels), (turned, turned), (aggregate,), cost=cost(1)
    )
    turned_got = swap(turned_send, "item", 1)
    turned_own, turned_send = call(
        halve,
        (struct((chips // 2,) + turned.shape[1:], F32), struct((chips // 2,) + turned.shape[1:], BF16)),
        (turned_keep, turned_got),
        cost=cost(0.1),
    )
    turned_got = swap(turned_send, "item", 2)

    hidden, slope = call(
        activate,
        (struct((share, hidden_width), BF16),) * 2,
        (pre_own, *pre_parts, cotangent),
        cost=cost(0.7),
    )
    far = [swap(slope, "item", 2 * k) for k in range(chips - 1, 0, -1)][::-1]
    *far, turned_got = lax.optimization_barrier((*far, turned_got))
    slope_pieces = []
    for piece in [slope, *far]:
        slope_pieces += [piece, swap(piece, "item", 1)]

    user_few = tile // user_size
    slopes, item_keep, item_send = call(
        functools.partial(backward, chips),
        (
            struct((group_rows, hidden_width), BF16),
            struct((user_size, chips, user_few, width), F32),
            struct((user_size, chips, user_few, width), BF16),
        ),
        (dense, level_weights, *slope_pieces),
        scratch=[pltpu.VMEM((levels * group_rows, width), BF16)],
        cost=cost(1.5),
    )
    item_got = swap(item_send, "item", 1)

    lanes = 128
    lane_blocks = min(hidden_width // lanes, user_size)
    few = part * lane_blocks // user_size
    rows = call(
        weight_rows,
        struct((user_size, chips // 2 * levels, few, lanes), F32),
        (slopes, turned_own, turned_got),
        scratch=[pltpu.VMEM((chips // 2 * levels * part, group_rows), BF16)],
        cost=cost(0.6),
    )

    def padded(amount):
        return -(-amount // 16) * 16

    blocks = width // lanes
    amount = padded(blocks * chips * user_few + chips // 2 * levels * few)
    mine, *sends = call(
        user_pieces,
        (struct((amount, lanes), F32),) + (struct((amount, lanes), BF16),) * (user_size - 1),
        (item_keep, item_got, rows),
        cost=cost(0.2),
    )
    parts = [swap(sends[k - 1], "user", k) for k in range(user_size - 1, 0, -1)][::-1]
    amount = padded(blocks * user_few + chips // 2 * levels * few)
    mine, *sends = call(
        functools.partial(chip_pieces, chips, user_few, blocks, chips // 2 * levels * few),
        (struct((amount, lanes), F32),) + (struct((amount, lanes), BF16),) * (chips - 1),
        (mine, *parts),
        scratch=[pltpu.VMEM((chips, blocks * user_few, lanes), F32)],
        cost=cost(0.1),
    )
    parts = [swap(sends[k - 1], "item", 2 * k) for k in range(chips - 1, 0, -1)][::-1]
    amount = padded(blocks * user_few + chips * levels * few)
    gathered = call(
        functools.partial(user_rows, blocks * user_few, levels * few),
        struct((amount, lanes), BF16),
        (mine, *parts),
        cost=cost(0.1),
    )
    gathered = [gathered] + [swap(gathered, "user", k) for k in range(user_size - 1, 0, -1)][::-1]
    others = [swap(piece, "item", 1) for piece in gathered]
    item_grad = call(
        functools.partial(item_rows, user_few), struct((tile, width), F32), gathered, cost=cost(0.7)
    )
    weight_grad = call(
        functools.partial(
            weight_out, chips, blocks * user_few, few, (group_rows * user_size) ** -0.5
        ),
        struct((levels, width, hidden_width), F32),
        (*gathered, *others),
        scratch=[pltpu.VMEM((2, chips, user_size, levels, few, lanes), F32)],
        cost=cost(1.3),
    )
    return hidden, item_grad, weight_grad


def solution(mesh):
    in_specs = (
        P("item", None),
        P(),
        P("user", "item", None, None, None),
        P("user", None),
        P("user", None),
        P(("user", "item"), None),
    )
    out_specs = (P(("user", "item"), None), P("item", None), P())
    return jax.shard_map(
        per_device, mesh=mesh, in_specs=in_specs, out_specs=out_specs, check_vma=False
    )
```

```python
import functools
import jax
import jax.numpy as jnp
from jax import lax
from jax.experimental import pallas as pl
from jax.experimental.pallas import tpu as pltpu
from jax.sharding import PartitionSpec as P

BF16 = jnp.bfloat16
F32 = jnp.float32
VMEM_LIMIT = 24 * 1024 * 1024


def partners(axis, step):
    return [(i, i ^ step) for i in range(lax.axis_size(axis))]


def swap(array, axis, step):
    return lax.ppermute(array, axis, partners(axis, step))


def tree_sum(parts):
    while len(parts) > 1:
        parts = [parts[i] + parts[i + 1] for i in range(0, len(parts), 2)]
    return parts[0]


def call(body, out_shapes, args, scratch=(), specs=None, cost=None):
    vmem = pl.BlockSpec(memory_space=pltpu.VMEM)
    return pl.pallas_call(
        body,
        out_shape=out_shapes,
        in_specs=specs if specs is not None else [vmem] * len(args),
        out_specs=jax.tree.map(lambda _: vmem, out_shapes),
        scratch_shapes=list(scratch),
        compiler_params=pltpu.CompilerParams(vmem_limit_bytes=VMEM_LIMIT),
        cost_estimate=cost,
    )(*args)


def cost(microseconds):
    return pl.CostEstimate(
        flops=int(microseconds * 1e9), bytes_accessed=int(microseconds * 3e6), transcendentals=0
    )


def struct(shape, dtype):
    return jax.ShapeDtypeStruct(shape, dtype)


def place_tiles(block_count, order, counts, mine, theirs, dense, sems):
    tile = mine.shape[-1]
    capacity, strips, _, share = mine.shape[1:5]
    chips = counts.shape[1] // 2
    user_blocks = chips // strips
    cell = lax.axis_index("item")
    dense[...] = jnp.zeros_like(dense)
    copies = []
    for other, tiles in enumerate((mine, theirs)):
        before = jnp.int32(0)
        for c in range(counts.shape[1]):
            before = before + jnp.where(c < (cell ^ other), counts[0, c], 0)
        holding = counts[0, cell ^ other]
        for t in range(capacity):
            copies.append((other, tiles, t, before, holding))

    def copy(number, strip):
        other, tiles, t, before, _ = copies[number]
        slot = order[0, jnp.minimum(before + t, order.shape[1] - 1)]
        target, block = slot // block_count, slot % block_count
        level, user_block = target // user_blocks, target % user_blocks
        row = (level * chips + user_block * strips + strip) * share
        column = ((block % 2) * chips + block // 2) * tile
        return pltpu.make_async_copy(
            tiles.at[0, t, strip],
            dense.at[:, pl.ds(pl.multiple_of(row, share), share),
                     pl.ds(pl.multiple_of(column, tile), tile)],
            sems.at[number * strips + strip],
        )

    for number, (_, _, t, _, holding) in enumerate(copies):
        @pl.when(t < holding)
        def _():
            for strip in range(strips):
                copy(number, strip).start()
    for number, (_, _, t, _, holding) in enumerate(copies):
        @pl.when(t < holding)
        def _():
            for strip in range(strips):
                copy(number, strip).wait()


def forward(chips, dense, weights, *refs):
    pieces = refs[: 2 * chips]
    features, own, *sends, pre = refs[2 * chips:]
    core = lax.axis_index("item") % 2
    chip = lax.axis_index("item") // 2
    levels, _, hidden = weights.shape
    tile = pieces[0].shape[0]
    for k in range(chips):
        for other in range(2):
            row = ((core ^ other) * chips + (chip ^ k)) * tile
            features[pl.ds(pl.multiple_of(row, tile), tile), :] = pieces[2 * k + other][...]
    rows = dense.shape[1] // levels
    total = jnp.zeros((rows, hidden), F32)
    for r in range(levels):
        block = jnp.dot(
            dense[core, r * rows:(r + 1) * rows, :], features[...], preferred_element_type=F32
        )
        total = total + jnp.dot(block.astype(BF16), weights[r], preferred_element_type=F32)
    pre[...] = total.reshape(pre.shape)
    own[...] = pre[chip]
    for k in range(1, chips):
        sends[k - 1][...] = pre[chip ^ k].astype(BF16)


def turn(levels, dense, features, own, send, turned):
    core = lax.axis_index("item") % 2
    chip = lax.axis_index("item") // 2
    chips, part, _ = turned.shape
    half = chips * part
    rows = dense.shape[1] // levels
    columns = features[:, pl.ds(pl.multiple_of(core * half, half), half)]
    for p in range(2):
        for r in range(levels):
            block = jnp.dot(
                dense[p, r * rows:(r + 1) * rows, :], columns, preferred_element_type=F32
            )
            at = (p * levels + r) * rows
            turned[:, :, at:at + rows] = block.T.reshape(chips, part, rows)
    for k in range(0, chips, 2):
        own[k // 2] = turned[chip ^ k]
        send[k // 2] = turned[chip ^ (k + 1)].astype(BF16)


def slopes_of(own, *refs):
    *parts, cotangent, pre_out, slope = refs
    pre = own[...]
    for part in parts:
        pre = pre + part[...].astype(F32)
    sigmoid = 1.0 / (1.0 + jnp.exp(-pre))
    pre_out[...] = pre
    slope[...] = (cotangent[...].astype(F32) * (sigmoid * (1.0 + pre * (1.0 - sigmoid)))).astype(BF16)


def activate(pre, hidden):
    hidden[...] = (pre[...] / (1.0 + jnp.exp(-pre[...]))).astype(BF16)


def backward(chips, other, dense, weights, *refs):
    pieces = refs[:chips]
    *before, slopes, items = refs[chips:]
    core = lax.axis_index("item") % 2
    chip = lax.axis_index("item") // 2
    levels, width, _ = weights.shape
    share = pieces[0].shape[0]
    for k in range(chips):
        slopes[pl.ds(pl.multiple_of((chip ^ k) * share, share), share), :] = pieces[k][...]
    rows = chips * share
    half = dense.shape[2] // 2
    columns = pl.ds(pl.multiple_of(core * half, half), half)
    total = jnp.zeros((half, width), F32)
    for r in range(levels):
        back = lax.dot_general(
            slopes[...], weights[r], (((1,), (1,)), ((), ())), preferred_element_type=F32
        ).astype(BF16)
        total = total + lax.dot_general(
            dense[core ^ other, r * rows:(r + 1) * rows, columns], back,
            (((0,), (0,)), ((), ())), preferred_element_type=F32,
        )
    total = total.reshape(items.shape)
    if before:
        total = total + before[0][...]
    items[...] = total


def weight_rows(levels, mine, theirs, keep, got, out, turned):
    core = lax.axis_index("item") % 2
    kept, part, columns = keep.shape
    rows = columns // (2 * levels)
    for k in range(kept):
        total = (keep[k] + got[k].astype(F32)).astype(BF16)
        for p in range(2):
            for r in range(levels):
                at, column = (k * levels + r) * part, (p * levels + r) * rows
                turned[p, at:at + part, :] = total[:, column:column + rows]
    terms = jnp.dot(turned[core], mine[...], preferred_element_type=F32)
    terms = terms + jnp.dot(turned[1 - core], theirs[...], preferred_element_type=F32)
    users, _, few, lanes = out.shape
    groups = part // few
    for u in range(users):
        for block in range(kept * levels):
            first = block * part + (u % groups) * few
            column = (u // groups) * lanes
            out[u, block] = terms[first:first + few, column:column + lanes]


def user_pieces(items, rows, *outs):
    user = lax.axis_index("user")
    chips, tile, width = items.shape
    users, blocks, part, lanes = rows.shape
    few = tile // users
    for k, out in enumerate(outs):
        first = pl.multiple_of((user ^ k) * few, few)
        at = 0
        for column in range(0, width, lanes):
            for z in range(chips):
                out[at:at + few] = items[z, pl.ds(first, few), column:column + lanes].astype(out.dtype)
                at += few
        for block in range(blocks):
            out[at:at + part] = rows[user ^ k, block].astype(out.dtype)
            at += part
        if at < out.shape[0]:
            out[at:] = jnp.zeros((out.shape[0] - at, lanes), out.dtype)


def chip_pieces(chips, few, blocks, rows, *refs):
    count = len(refs) - chips - 1
    parts, outs, total = refs[:count], refs[count:-1], refs[-1]
    chip = lax.axis_index("item") // 2
    summed = parts[0][...]
    for part in parts[1:]:
        summed = summed + part[...].astype(F32)
    for block in range(blocks):
        for z in range(chips):
            at = (block * chips + z) * few
            total[z, block * few:(block + 1) * few] = summed[at:at + few]
    first = blocks * chips * few
    weight = summed[first:first + rows].astype(BF16)
    for k, out in enumerate(outs):
        out[:blocks * few] = total[chip ^ k].astype(out.dtype)
        out[blocks * few:blocks * few + rows] = weight.astype(out.dtype)
        if blocks * few + rows < out.shape[0]:
            out[blocks * few + rows:] = jnp.zeros((out.shape[0] - blocks * few - rows, out.shape[1]), out.dtype)


def user_rows(items, rows, *refs):
    own, *parts, out = refs
    parts = [own, *parts[::-1]]
    total = parts[0][:items]
    for part in parts[1:]:
        total = total + part[:items].astype(F32)
    out[:items] = total.astype(BF16)
    for k in range(len(parts)):
        terms = []
        for j in range(k % 2, len(parts), 2):
            at = items + ((j ^ k) // 2) * rows
            terms.append(parts[j][at:at + rows].astype(BF16).astype(F32))
        out[items + k * rows:items + (k + 1) * rows] = tree_sum(terms).astype(BF16)
    if items + len(parts) * rows < out.shape[0]:
        out[items + len(parts) * rows:] = jnp.zeros((out.shape[0] - items - len(parts) * rows, out.shape[1]), BF16)


def item_rows(few, *refs):
    *parts, out = refs
    user = lax.axis_index("user")
    lanes = parts[0].shape[1]
    for k, part in enumerate(parts):
        row = pl.multiple_of((user ^ k) * few, few)
        for block in range(out.shape[1] // lanes):
            out[pl.ds(row, few), block * lanes:(block + 1) * lanes] = part[block * few:(block + 1) * few].astype(F32)


def weight_out(chips, items, few, scale, *refs):
    *pieces, out, wide = refs
    core = lax.axis_index("item") % 2
    chip = lax.axis_index("item") // 2
    user = lax.axis_index("user")
    levels, width, _ = out.shape
    lanes = pieces[0].shape[1]
    users = len(pieces) // 2
    part = width // (2 * chips)
    groups = part // few
    for other in range(2):
        for j in range(users):
            piece = pieces[users * other + j]
            for k in range(chips):
                at = items + k * levels * few
                for r in range(levels):
                    block = piece[at + r * few:at + (r + 1) * few].astype(F32) * scale
                    if groups == 1 and few % 8 == 0:
                        row = (core ^ other) * (width // 2) + (chip ^ k) * part
                        column = (user ^ j) * lanes
                        out[r, pl.ds(pl.multiple_of(row, few), few),
                            pl.ds(pl.multiple_of(column, lanes), lanes)] = block
                    else:
                        wide[core ^ other, chip ^ k, user ^ j, r] = block
    if not (groups == 1 and few % 8 == 0):
        for c in range(2):
            for z in range(chips):
                for u in range(users):
                    row = c * (width // 2) + z * part + (u % groups) * few
                    column = (u // groups) * lanes
                    for r in range(levels):
                        out[r, row:row + few, column:column + lanes] = wide[c, z, u, r]


def per_device(item_features, level_weights, tile_values, tile_order, tile_counts, cotangent):
    item_size = lax.axis_size("item")
    user_size = lax.axis_size("user")
    chips = item_size // 2
    levels, width, hidden_width = level_weights.shape
    tile = tile_values.shape[-1]
    capacity = tile_values.shape[2]
    local_items = item_features.shape[0]
    items = local_items * item_size
    block_count = items // tile
    user_blocks = tile_order.shape[1] // (levels * block_count)
    group_rows = user_blocks * tile
    share = group_rows // item_size
    smem = pl.BlockSpec(memory_space=pltpu.SMEM)

    strips = tile // (2 * share)
    tiles = tile_values.reshape(1, capacity, strips, 2, share, tile)
    other_tiles = swap(tiles, "item", 1)
    far = [swap(item_features, "item", 2 * k) for k in range(chips - 1, 0, -1)][::-1]
    rows = levels * chips * share
    dense = call(
        functools.partial(place_tiles, block_count),
        struct((2, rows, items), BF16),
        (tile_order, tile_counts, tiles, other_tiles),
        scratch=[pltpu.SemaphoreType.DMA((2 * capacity * strips,))],
        specs=[smem, smem, pl.BlockSpec(memory_space=pl.ANY), pl.BlockSpec(memory_space=pl.ANY)],
        cost=cost(4),
    )
    *far, dense = lax.optimization_barrier((*far, dense))
    feature_pieces = []
    for piece in [item_features, *far]:
        feature_pieces += [piece, swap(piece, "item", 1)]

    features, pre_own, *pre_sends = call(
        functools.partial(forward, chips),
        (struct((items, width), BF16), struct((share, hidden_width), F32))
        + (struct((share, hidden_width), BF16),) * (chips - 1),
        (dense, level_weights, *feature_pieces),
        scratch=[pltpu.VMEM((chips, share, hidden_width), F32)],
        cost=cost(1.5),
    )
    pre_parts = [swap(pre_sends[k - 1], "item", 2 * k) for k in range(1, chips)]

    part = width // item_size
    kept = chips // 2
    turned_own, turned_send = call(
        functools.partial(turn, levels),
        (struct((kept, part, 2 * rows), F32), struct((kept, part, 2 * rows), BF16)),
        (dense, features),
        scratch=[pltpu.VMEM((chips, part, 2 * rows), F32)],
        cost=cost(3),
    )
    turned_got = swap(turned_send, "item", 2)

    pre, slope = call(
        slopes_of,
        (struct((share, hidden_width), F32), struct((share, hidden_width), BF16)),
        (pre_own, *pre_parts[::-1], cotangent),
        cost=cost(0.1),
    )
    far = [swap(slope, "item", 2 * k) for k in range(chips - 1, 0, -1)][::-1]
    hidden = call(activate, struct((share, hidden_width), BF16), (pre,), cost=cost(0.7))
    mine = [slope, *far]
    theirs = [swap(piece, "item", 1) for piece in mine]
    *theirs, turned_got = lax.optimization_barrier((*theirs, turned_got))

    item_terms = struct((chips, tile, width), F32)
    half_slopes = struct((group_rows // 2, hidden_width), BF16)
    my_slopes, item_part = call(
        functools.partial(backward, chips, 0),
        (half_slopes, item_terms),
        (dense, level_weights, *mine),
        cost=cost(1),
    )
    their_slopes, item_part = call(
        functools.partial(backward, chips, 1),
        (half_slopes, item_terms),
        (dense, level_weights, *theirs, item_part),
        cost=cost(1),
    )

    user_few = tile // user_size
    lanes = 128
    lane_blocks = min(hidden_width // lanes, user_size)
    few = part * lane_blocks // user_size
    weight_part = call(
        functools.partial(weight_rows, levels),
        struct((user_size, kept * levels, few, lanes), F32),
        (my_slopes, their_slopes, turned_own, turned_got),
        scratch=[pltpu.VMEM((2, kept * levels * part, group_rows // 2), BF16)],
        cost=cost(0.6),
    )

    def padded(amount):
        return -(-amount // 16) * 16

    blocks = width // lanes
    amount = padded(blocks * chips * user_few + chips // 2 * levels * few)
    mine, *sends = call(
        user_pieces,
        (struct((amount, lanes), F32),) + (struct((amount, lanes), BF16),) * (user_size - 1),
        (item_part, weight_part),
        cost=cost(0.2),
    )
    parts = [swap(sends[k - 1], "user", k) for k in range(user_size - 1, 0, -1)][::-1]
    amount = padded(blocks * user_few + chips // 2 * levels * few)
    mine, *sends = call(
        functools.partial(chip_pieces, chips, user_few, blocks, chips // 2 * levels * few),
        (struct((amount, lanes), F32),) + (struct((amount, lanes), BF16),) * (chips - 1),
        (mine, *parts[::-1]),
        scratch=[pltpu.VMEM((chips, blocks * user_few, lanes), F32)],
        cost=cost(0.1),
    )
    parts = [swap(sends[k - 1], "item", 2 * k) for k in range(chips - 1, 0, -1)][::-1]
    amount = padded(blocks * user_few + chips * levels * few)
    gathered = call(
        functools.partial(user_rows, blocks * user_few, levels * few),
        struct((amount, lanes), BF16),
        (mine, *parts[::-1]),
        cost=cost(0.1),
    )
    gathered = [gathered] + [swap(gathered, "user", k) for k in range(user_size - 1, 0, -1)][::-1]
    others = [swap(piece, "item", 1) for piece in gathered]
    item_grad = call(
        functools.partial(item_rows, user_few), struct((tile, width), F32), gathered, cost=cost(0.7)
    )
    weight_grad = call(
        functools.partial(
            weight_out, chips, blocks * user_few, few, (group_rows * user_size) ** -0.5
        ),
        struct((levels, width, hidden_width), F32),
        (*gathered, *others),
        scratch=[pltpu.VMEM((2, chips, user_size, levels, few, lanes), F32)],
        cost=cost(1.3),
    )
    return hidden, item_grad, weight_grad


def solution(mesh):
    in_specs = (
        P("item", None),
        P(),
        P("user", "item", None, None, None),
        P("user", None),
        P("user", None),
        P(("user", "item"), None),
    )
    out_specs = (P(("user", "item"), None), P("item", None), P())
    return jax.shard_map(
        per_device, mesh=mesh, in_specs=in_specs, out_specs=out_specs, check_vma=False
    )
```

```python
import functools
import jax
import jax.numpy as jnp
from jax import lax
from jax.experimental import pallas as pl
from jax.experimental.pallas import tpu as pltpu
from jax.sharding import PartitionSpec as P

BF16 = jnp.bfloat16
F32 = jnp.float32
VMEM_LIMIT = 24 * 1024 * 1024
LANES = 128


def swap(array, axis, step):
    return lax.ppermute(array, axis, [(i, i ^ step) for i in range(lax.axis_size(axis))])


def swap_each(arrays, axis, unit):
    return [swap(array, axis, (k + 1) * unit) for k, array in enumerate(arrays)]


def by_reach(parts):
    return [parts[k - 1] for k in reach(len(parts))]


def reach(count):
    return sorted(range(1, count + 1), reverse=True)


def together(parts, *others):
    ks = reach(len(parts))[::-1]
    out = lax.optimization_barrier((*[parts[k - 1] for k in ks], *others))
    made = dict(zip(ks, out))
    return [made[k] for k in sorted(made)], *out[len(ks):]


def tree_sum(parts):
    while len(parts) > 1:
        parts = [parts[i] + parts[i + 1] for i in range(0, len(parts), 2)]
    return parts[0]


def cost(microseconds):
    return pl.CostEstimate(
        flops=int(microseconds * 1e9), bytes_accessed=int(microseconds * 3e6), transcendentals=0
    )


def struct(shape, dtype):
    return jax.ShapeDtypeStruct(shape, dtype)


def space(memory_space):
    return pl.BlockSpec(memory_space=memory_space)


def call(body, outs, args, time, scratch=(), specs=None, out_specs=None, aliases=None):
    vmem = space(pltpu.VMEM)
    return pl.pallas_call(
        body,
        out_shape=outs,
        in_specs=specs or [vmem] * len(args),
        out_specs=out_specs or jax.tree.map(lambda _: vmem, outs),
        scratch_shapes=list(scratch),
        compiler_params=pltpu.CompilerParams(vmem_limit_bytes=VMEM_LIMIT),
        cost_estimate=cost(time),
        input_output_aliases=aliases or {},
    )(*args)


def here():
    item = lax.axis_index("item")
    return item // 2, item % 2


def place_tiles(block_count, order, counts, mine, theirs, dense, order_s, counts_s, sems):
    tile = mine.shape[-1]
    capacity, strips, _, share = mine.shape[1:5]
    chips = counts.shape[1] // 2
    user_blocks = chips // strips
    scalars = [
        pltpu.make_async_copy(order, order_s, sems.at[2 * capacity * strips]),
        pltpu.make_async_copy(counts, counts_s, sems.at[2 * capacity * strips + 1]),
    ]
    for scalar in scalars:
        scalar.start()
    dense[...] = jnp.zeros_like(dense)
    for scalar in scalars:
        scalar.wait()
    copies = []
    for other, tiles in enumerate((mine, theirs)):
        cell = lax.axis_index("item") ^ other
        before = jnp.int32(0)
        for c in range(counts.shape[1]):
            before = before + jnp.where(c < cell, counts_s[0, c], 0)
        holding = counts_s[0, cell]
        for t in range(capacity):
            copies.append((other * capacity + t, tiles, t, before, holding))

    def copy(number, tiles, t, before, strip):
        slot = order_s[0, jnp.minimum(before + t, order.shape[1] - 1)]
        target, block = slot // block_count, slot % block_count
        level, user_block = target // user_blocks, target % user_blocks
        row = (level * chips + user_block * strips + strip) * share
        column = ((block % 2) * chips + block // 2) * tile
        return pltpu.make_async_copy(
            tiles.at[0, t, strip],
            dense.at[:, pl.ds(pl.multiple_of(row, share), share),
                     pl.ds(pl.multiple_of(column, tile), tile)],
            sems.at[number * strips + strip],
        )

    for number, tiles, t, before, holding in copies:
        @pl.when(t < holding)
        def _():
            for strip in range(strips):
                copy(number, tiles, t, before, strip).start()
    for number, tiles, t, before, holding in copies:
        @pl.when(t < holding)
        def _():
            for strip in range(strips):
                copy(number, tiles, t, before, strip).wait()


def forward(chips, dense, weights, *refs):
    pieces = refs[: 2 * chips]
    features, own, *sends, pre = refs[2 * chips:]
    chip, core = here()
    levels, _, hidden = weights.shape
    tile = pieces[0].shape[0]
    for k in range(chips):
        for other in range(2):
            row = ((core ^ other) * chips + (chip ^ k)) * tile
            features[pl.ds(pl.multiple_of(row, tile), tile), :] = pieces[2 * k + other][...]
    rows = dense.shape[1] // levels
    total = jnp.zeros((rows, hidden), F32)
    for r in range(levels):
        block = jnp.dot(
            dense[core, r * rows:(r + 1) * rows, :], features[...], preferred_element_type=F32
        )
        total = total + jnp.dot(block.astype(BF16), weights[r], preferred_element_type=F32)
    pre[...] = total.reshape(pre.shape)
    own[...] = pre[chip]
    for k in range(1, chips):
        sends[k - 1][...] = pre[chip ^ k].astype(BF16)


def turn(levels, dense, features, own, send, turned):
    chip, core = here()
    chips, part, _ = turned.shape
    half = chips * part
    rows = dense.shape[1] // levels
    columns = features[:, pl.ds(pl.multiple_of(core * half, half), half)]
    for p in range(2):
        for r in range(levels):
            block = jnp.dot(
                dense[p, r * rows:(r + 1) * rows, :], columns, preferred_element_type=F32
            )
            at = (p * levels + r) * rows
            turned[:, :, at:at + rows] = block.T.reshape(chips, part, rows)
    for k in range(0, chips, 2):
        own[k // 2] = turned[chip ^ k]
        send[k // 2] = turned[chip ^ (k + 1)].astype(BF16)


def slopes_of(own, *refs):
    *parts, cotangent, pre_out, slope = refs
    pre = own[...]
    for part in parts:
        pre = pre + part[...].astype(F32)
    sigmoid = 1.0 / (1.0 + jnp.exp(-pre))
    pre_out[...] = pre
    slope[...] = (cotangent[...].astype(F32) * (sigmoid * (1.0 + pre * (1.0 - sigmoid)))).astype(BF16)


def activate(pre, hidden):
    hidden[...] = (pre[...] / (1.0 + jnp.exp(-pre[...]))).astype(BF16)


def item_terms(chips, other, dense, weights, pieces, slopes):
    chip, core = here()
    levels, width, _ = weights.shape
    share = pieces[0].shape[0]
    for k in range(chips):
        slopes[pl.ds(pl.multiple_of((chip ^ k) * share, share), share), :] = pieces[k][...]
    rows = chips * share
    half = dense.shape[2] // 2
    columns = pl.ds(pl.multiple_of(core * half, half), half)
    total = jnp.zeros((half, width), F32)
    for r in range(levels):
        back = lax.dot_general(
            slopes[...], weights[r], (((1,), (1,)), ((), ())), preferred_element_type=F32
        ).astype(BF16)
        total = total + lax.dot_general(
            dense[core ^ other, r * rows:(r + 1) * rows, columns], back,
            (((0,), (0,)), ((), ())), preferred_element_type=F32,
        )
    return total


def backward_mine(chips, dense, weights, *refs):
    *pieces, out, slopes = refs
    out[...] = item_terms(chips, 0, dense, weights, pieces, slopes).reshape(out.shape)


def backward_theirs(chips, few, dense, weights, *refs):
    mine, theirs = refs[:chips], refs[chips:2 * chips]
    before, keep, got, *outs, their_slopes, items, turned, slopes, chunks = refs[2 * chips:]
    chip, core = here()
    user = lax.axis_index("user")
    levels = weights.shape[0]
    terms = item_terms(chips, 1, dense, weights, theirs, their_slopes)
    items[...] = before[...] + terms.reshape(items.shape)

    share = mine[0].shape[0]
    kept, part, columns = keep.shape
    rows = columns // (2 * levels)
    for k in range(chips):
        for other, pieces in enumerate((mine, theirs)):
            row = ((core ^ other) * chips + (chip ^ k)) * share
            slopes[pl.ds(pl.multiple_of(row, share), share), :] = pieces[k][...]
    for k in range(kept):
        total = (keep[k] + got[k].astype(F32)).astype(BF16)
        for p in range(2):
            for r in range(levels):
                at, column = (k * levels + r) * part, (p * levels + r) * rows
                turned[at:at + part, p * rows:(p + 1) * rows] = total[:, column:column + rows]
    terms = jnp.dot(turned[...], slopes[...], preferred_element_type=F32)
    users = chunks.shape[0]
    groups = part // few
    for u in range(users):
        for block in range(kept * levels):
            first = block * part + (u % groups) * few
            column = (u // groups) * LANES
            chunks[u, block * few:(block + 1) * few] = terms[first:first + few, column:column + LANES]

    _, tile, width = items.shape
    item_few = tile // users
    for k, out in enumerate(outs):
        first = pl.multiple_of((user ^ k) * item_few, item_few)
        blocks = [
            items[z, pl.ds(first, item_few), column:column + LANES]
            for column in range(0, width, LANES)
            for z in range(chips)
        ]
        fill(out, *blocks, chunks[user ^ k])


def fill(out, *blocks):
    at = 0
    for block in blocks:
        out[at:at + block.shape[0]] = block.astype(out.dtype)
        at += block.shape[0]
    if at < out.shape[0]:
        out[at:] = jnp.zeros((out.shape[0] - at,) + out.shape[1:], out.dtype)


def user_sum(chips, few, blocks, rows, *refs):
    count = len(refs) - chips - 1
    parts, outs, total = refs[:count], refs[count:-1], refs[-1]
    chip, _ = here()
    summed = parts[0][...]
    for part in parts[1:]:
        summed = summed + part[...].astype(F32)
    for block in range(blocks):
        for z in range(chips):
            at = (block * chips + z) * few
            total[z, block * few:(block + 1) * few] = summed[at:at + few]
    first = blocks * chips * few
    weight = summed[first:first + rows].astype(BF16)
    for k, out in enumerate(outs):
        fill(out, total[chip ^ k], weight)


def line_sum(items, rows, stride, own, *refs):
    *parts, out = refs
    made = dict(zip(reach(len(parts)), parts))
    parts = [own] + [made[k] for k in sorted(made)]
    total = own[:items]
    for part in parts[1:]:
        total = total + part[:items].astype(F32)
    blocks = [total]
    for k in range(len(parts)):
        terms = []
        for j in range(k % stride, len(parts), stride):
            at = items + ((j ^ k) // stride) * rows
            terms.append(parts[j][at:at + rows].astype(BF16).astype(F32))
        blocks.append(tree_sum(terms))
    fill(out, *blocks)


def weight_out(chips, items, few, other, scale, *refs):
    *pieces, out, wide, loose, item_rows, sems = refs
    if other:
        pieces = pieces[:-1]
    else:
        *pieces, item_grad = pieces
    chip, core = here()
    user = lax.axis_index("user")
    levels, half, _ = wide.shape
    users = len(pieces)
    part = half // chips
    groups = part // few
    copies = []
    if not other:
        item_few = item_rows.shape[0] // users
        for j in range(users):
            row = pl.multiple_of((user ^ j) * item_few, item_few)
            for block in range(items // item_few):
                item_rows[pl.ds(row, item_few), block * LANES:(block + 1) * LANES] = (
                    pieces[j][block * item_few:(block + 1) * item_few].astype(F32)
                )
        copies.append(pltpu.make_async_copy(item_rows, item_grad, sems.at[levels]))
        copies[-1].start()
    for r in range(levels):
        for j in range(users):
            for k in range(chips):
                at = items + (k * levels + r) * few
                block = pieces[j][at:at + few].astype(F32) * scale
                if groups == 1:
                    row = pl.multiple_of((chip ^ k) * part, part)
                    column = pl.multiple_of((user ^ j) * LANES, LANES)
                    wide[r, pl.ds(row, part), pl.ds(column, LANES)] = block
                else:
                    loose[chip ^ k, user ^ j] = block
        if groups > 1:
            for z in range(chips):
                for u in range(users):
                    row, column = z * part + (u % groups) * few, (u // groups) * LANES
                    wide[r, row:row + few, column:column + LANES] = loose[z, u]
        first = pl.multiple_of((core ^ other) * half, half)
        copies.append(pltpu.make_async_copy(wide.at[r], out.at[r, pl.ds(first, half), :], sems.at[r]))
        copies[-1].start()
    for copy in copies:
        copy.wait()


def per_device(item_features, level_weights, tile_values, tile_order, tile_counts, cotangent):
    item_size = lax.axis_size("item")
    user_size = lax.axis_size("user")
    chips = item_size // 2
    levels, width, hidden_width = level_weights.shape
    tile = tile_values.shape[-1]
    capacity = tile_values.shape[2]
    items = item_features.shape[0] * item_size
    block_count = items // tile
    user_blocks = tile_order.shape[1] // (levels * block_count)
    group_rows = user_blocks * tile
    share = group_rows // item_size
    rows = levels * chips * share
    vmem, anywhere = space(pltpu.VMEM), space(pl.ANY)

    strips = tile // (2 * share)
    tiles = tile_values.reshape(1, capacity, strips, 2, share, tile)
    other_tiles = swap(tiles, "item", 1)
    far = swap_each([item_features] * (chips - 1), "item", 2)
    dense = call(
        functools.partial(place_tiles, block_count),
        struct((2, rows, items), BF16),
        (tile_order, tile_counts, tiles, other_tiles),
        4,
        scratch=[
            pltpu.SMEM(tile_order.shape, jnp.int32),
            pltpu.SMEM(tile_counts.shape, jnp.int32),
            pltpu.SemaphoreType.DMA((2 * capacity * strips + 2,)),
        ],
        specs=[space(pltpu.HBM)] * 3 + [anywhere],
    )
    far, dense = together(far, dense)
    feature_pieces = []
    for piece in [item_features, *far]:
        feature_pieces += [piece, swap(piece, "item", 1)]

    piece = struct((share, hidden_width), BF16)
    features, pre_own, *pre_sends = call(
        functools.partial(forward, chips),
        (struct((items, width), BF16), struct((share, hidden_width), F32)) + (piece,) * (chips - 1),
        (dense, level_weights, *feature_pieces),
        1.5,
        scratch=[pltpu.VMEM((chips, share, hidden_width), F32)],
    )
    pre_parts = swap_each(pre_sends, "item", 2)

    part = width // item_size
    kept = chips // 2
    turned_own, turned_send = call(
        functools.partial(turn, levels),
        (struct((kept, part, 2 * rows), F32), struct((kept, part, 2 * rows), BF16)),
        (dense, features),
        3,
        scratch=[pltpu.VMEM((chips, part, 2 * rows), F32)],
    )
    turned_got = swap(turned_send, "item", 2)

    pre, slope = call(
        slopes_of,
        (struct((share, hidden_width), F32), piece),
        (pre_own, *by_reach(pre_parts), cotangent),
        0.1,
    )
    far = swap_each([slope] * (chips - 1), "item", 2)
    hidden = call(activate, piece, (pre,), 0.7)
    mine = [slope, *far]
    theirs = [swap(piece, "item", 1) for piece in mine]
    *theirs, turned_got = lax.optimization_barrier((*theirs, turned_got))

    item_part = call(
        functools.partial(backward_mine, chips),
        struct((chips, tile, width), F32),
        (dense, level_weights, *mine),
        1,
        scratch=[pltpu.VMEM((chips * share, hidden_width), BF16)],
    )

    def padded(amount):
        return -(-amount // 16) * 16

    few = part * min(hidden_width // LANES, user_size) // user_size
    item_few = tile // user_size
    blocks = width // LANES
    count = kept * levels * few
    amount = padded(blocks * chips * item_few + count)
    own, *sends = call(
        functools.partial(backward_theirs, chips, few),
        (struct((amount, LANES), F32),) + (struct((amount, LANES), BF16),) * (user_size - 1),
        (dense, level_weights, *mine, *theirs, item_part, turned_own, turned_got),
        1.3,
        scratch=[
            pltpu.VMEM((chips * share, hidden_width), BF16),
            pltpu.VMEM((chips, tile, width), F32),
            pltpu.VMEM((kept * levels * part, group_rows), BF16),
            pltpu.VMEM((group_rows, hidden_width), BF16),
            pltpu.VMEM((user_size, count, LANES), F32),
        ],
    )
    parts = swap_each(sends, "user", 1)
    parts, hidden = together(parts, hidden)
    amount = padded(blocks * item_few + count)
    own, *sends = call(
        functools.partial(user_sum, chips, item_few, blocks, count),
        (struct((amount, LANES), F32),) + (struct((amount, LANES), BF16),) * (chips - 1),
        (own, *parts[::-1]),
        0.1,
        scratch=[pltpu.VMEM((chips, blocks * item_few, LANES), F32)],
    )
    parts = swap_each(sends, "item", 2)
    amount = padded(blocks * item_few + chips * levels * few)
    gathered = call(
        functools.partial(line_sum, blocks * item_few, levels * few, chips // kept),
        struct((amount, LANES), BF16),
        (own, *by_reach(parts)),
        0.1,
    )
    gathered = [gathered] + swap_each([gathered] * (user_size - 1), "user", 1)
    others = [swap(piece, "item", 1) for piece in gathered]
    weight_grad = struct((levels, width, hidden_width), F32)
    scratch = [
        pltpu.VMEM((levels, width // 2, hidden_width), F32),
        pltpu.VMEM((chips, user_size, few, LANES), F32),
        pltpu.VMEM((tile, width), F32),
        pltpu.SemaphoreType.DMA((levels + 1,)),
    ]
    scale = (group_rows * user_size) ** -0.5
    item_grad, half_grad = call(
        functools.partial(weight_out, chips, blocks * item_few, few, 0, scale),
        (struct((tile, width), F32), weight_grad),
        gathered,
        0.9,
        scratch=scratch,
        out_specs=(anywhere, anywhere),
    )
    weight_grad = call(
        functools.partial(weight_out, chips, blocks * item_few, few, 1, scale),
        weight_grad,
        (*others, half_grad),
        0.9,
        scratch=scratch,
        specs=[vmem] * user_size + [anywhere],
        out_specs=anywhere,
        aliases={user_size: 0},
    )
    return hidden, item_grad, weight_grad


def solution(mesh):
    in_specs = (
        P("item", None),
        P(),
        P("user", "item", None, None, None),
        P("user", None),
        P("user", None),
        P(("user", "item"), None),
    )
    out_specs = (P(("user", "item"), None), P("item", None), P())
    return jax.shard_map(
        per_device, mesh=mesh, in_specs=in_specs, out_specs=out_specs, check_vma=False
    )
```

```python
import functools
import jax
import jax.numpy as jnp
from jax import lax
from jax.experimental import pallas as pl
from jax.experimental.pallas import tpu as pltpu
from jax.sharding import PartitionSpec as P

BF16 = jnp.bfloat16
F32 = jnp.float32
VMEM_LIMIT = 24 * 1024 * 1024
LANES = 128


def swap(array, axis, step):
    return lax.ppermute(array, axis, [(i, i ^ step) for i in range(lax.axis_size(axis))])


def swap_each(arrays, axis, unit):
    return [swap(array, axis, (k + 1) * unit) for k, array in enumerate(arrays)]


def by_reach(parts):
    return [parts[k - 1] for k in reach(len(parts))]


def reach(count):
    return sorted(range(1, count + 1), reverse=True)


def together(parts, *others):
    ks = reach(len(parts))[::-1]
    out = lax.optimization_barrier((*[parts[k - 1] for k in ks], *others))
    made = dict(zip(ks, out))
    return [made[k] for k in sorted(made)], *out[len(ks):]


def tree_sum(parts):
    while len(parts) > 1:
        parts = [parts[i] + parts[i + 1] for i in range(0, len(parts), 2)]
    return parts[0]


def cost(microseconds):
    return pl.CostEstimate(
        flops=int(microseconds * 1e9), bytes_accessed=int(microseconds * 3e6), transcendentals=0
    )


def struct(shape, dtype):
    return jax.ShapeDtypeStruct(shape, dtype)


def space(memory_space):
    return pl.BlockSpec(memory_space=memory_space)


def call(body, outs, args, time, scratch=(), specs=None, out_specs=None, aliases=None):
    vmem = space(pltpu.VMEM)
    return pl.pallas_call(
        body,
        out_shape=outs,
        in_specs=specs or [vmem] * len(args),
        out_specs=out_specs or jax.tree.map(lambda _: vmem, outs),
        scratch_shapes=list(scratch),
        compiler_params=pltpu.CompilerParams(vmem_limit_bytes=VMEM_LIMIT),
        cost_estimate=cost(time),
        input_output_aliases=aliases or {},
    )(*args)


def here():
    item = lax.axis_index("item")
    return item // 2, item % 2


def place_tiles(block_count, order, counts, mine, theirs, dense, order_s, counts_s, sems):
    tile = mine.shape[-1]
    capacity, strips, _, share = mine.shape[1:5]
    chips = counts.shape[1] // 2
    user_blocks = chips // strips
    scalars = [
        pltpu.make_async_copy(order, order_s, sems.at[2 * capacity * strips]),
        pltpu.make_async_copy(counts, counts_s, sems.at[2 * capacity * strips + 1]),
    ]
    for scalar in scalars:
        scalar.start()
    dense[...] = jnp.zeros_like(dense)
    for scalar in scalars:
        scalar.wait()
    copies = []
    for other, tiles in enumerate((mine, theirs)):
        cell = lax.axis_index("item") ^ other
        before = jnp.int32(0)
        for c in range(counts.shape[1]):
            before = before + jnp.where(c < cell, counts_s[0, c], 0)
        holding = counts_s[0, cell]
        for t in range(capacity):
            copies.append((other * capacity + t, tiles, t, before, holding))

    def copy(number, tiles, t, before, strip):
        slot = order_s[0, jnp.minimum(before + t, order.shape[1] - 1)]
        target, block = slot // block_count, slot % block_count
        level, user_block = target // user_blocks, target % user_blocks
        row = (level * chips + user_block * strips + strip) * share
        column = ((block % 2) * chips + block // 2) * tile
        return pltpu.make_async_copy(
            tiles.at[0, t, strip],
            dense.at[:, pl.ds(pl.multiple_of(row, share), share),
                     pl.ds(pl.multiple_of(column, tile), tile)],
            sems.at[number * strips + strip],
        )

    for number, tiles, t, before, holding in copies:
        @pl.when(t < holding)
        def _():
            for strip in range(strips):
                copy(number, tiles, t, before, strip).start()
    for number, tiles, t, before, holding in copies:
        @pl.when(t < holding)
        def _():
            for strip in range(strips):
                copy(number, tiles, t, before, strip).wait()


def stack(pieces, out):
    chip, _ = here()
    size = pieces[0].shape[0]
    for k, piece in enumerate(pieces):
        out[pl.ds(pl.multiple_of((chip ^ k) * size, size), size), :] = piece[...]


def columns_of(dense, parity):
    half = dense.shape[2] // 2
    return pl.ds(pl.multiple_of(parity * half, half), half)


def forward_mine(dense, *refs):
    *pieces, features, terms = refs
    _, core = here()
    stack(pieces, features)
    terms[...] = jnp.dot(
        dense[core, :, columns_of(dense, core)], features[...], preferred_element_type=F32
    )


def forward_theirs(chips, dense, weights, *refs):
    pieces = refs[:chips]
    before, features, own, *sends, pre = refs[chips:]
    chip, core = here()
    levels, _, hidden = weights.shape
    stack(pieces, features)
    rows = dense.shape[1] // levels
    total = jnp.zeros((rows, hidden), F32)
    for r in range(levels):
        at = pl.ds(r * rows, rows)
        block = before[at, :] + jnp.dot(
            dense[core, at, columns_of(dense, 1 - core)], features[...], preferred_element_type=F32
        )
        total = total + jnp.dot(block.astype(BF16), weights[r], preferred_element_type=F32)
    pre[...] = total.reshape(pre.shape)
    own[...] = pre[chip]
    for k in range(1, chips):
        sends[k - 1][...] = pre[chip ^ k].astype(BF16)


def turn(levels, dense, mine, theirs, own, send, turned):
    chip, core = here()
    chips, part, _ = turned.shape
    half = chips * part
    rows = dense.shape[1] // levels
    width = pl.ds(pl.multiple_of(core * half, half), half)
    for p in range(2):
        for r in range(levels):
            at = p * levels * rows + r * rows
            block = jnp.zeros((rows, half), F32)
            for parity, features in ((core, mine), (1 - core, theirs)):
                block = block + jnp.dot(
                    dense[p, pl.ds(r * rows, rows), columns_of(dense, parity)],
                    features[:, width],
                    preferred_element_type=F32,
                )
            turned[:, :, at:at + rows] = block.T.reshape(chips, part, rows)
    for k in range(0, chips, 2):
        own[k // 2] = turned[chip ^ k]
        send[k // 2] = turned[chip ^ (k + 1)].astype(BF16)


def flip(dense, weights, flipped, weights_t):
    _, core = here()
    step = dense.shape[1] // weights.shape[0]
    for r in range(weights.shape[0]):
        weights_t[r] = weights[r].T
        for p in range(2):
            at = pl.ds(r * step, step)
            flipped[p, :, at] = dense[p, at, columns_of(dense, core)].T


def slopes_of(own, *refs):
    *parts, cotangent, pre_out, slope = refs
    pre = own[...]
    for part in parts:
        pre = pre + part[...].astype(F32)
    sigmoid = 1.0 / (1.0 + jnp.exp(-pre))
    pre_out[...] = pre
    slope[...] = (cotangent[...].astype(F32) * (sigmoid * (1.0 + pre * (1.0 - sigmoid)))).astype(BF16)


def activate(pre, hidden):
    hidden[...] = (pre[...] / (1.0 + jnp.exp(-pre[...]))).astype(BF16)


def item_terms(other, flipped, weights_t, pieces, slopes, back):
    _, core = here()
    stack(pieces, slopes)
    rows = slopes.shape[0]
    for r in range(weights_t.shape[0]):
        back[r * rows:(r + 1) * rows, :] = jnp.dot(
            slopes[...], weights_t[r], preferred_element_type=F32
        ).astype(BF16)
    return jnp.dot(flipped[core ^ other], back[...], preferred_element_type=F32)


def backward_mine(flipped, weights_t, *refs):
    *pieces, out, slopes, back = refs
    out[...] = item_terms(0, flipped, weights_t, pieces, slopes, back).reshape(out.shape)


def backward_theirs(chips, few, flipped, weights_t, *refs):
    mine, theirs = refs[:chips], refs[chips:2 * chips]
    before, keep, got, *outs, their_slopes, back, items, turned, slopes, chunks = refs[2 * chips:]
    chip, core = here()
    user = lax.axis_index("user")
    levels = weights_t.shape[0]
    terms = item_terms(1, flipped, weights_t, theirs, their_slopes, back)
    items[...] = before[...] + terms.reshape(items.shape)

    share = mine[0].shape[0]
    kept, part, columns = keep.shape
    rows = columns // (2 * levels)
    for k in range(chips):
        for other, pieces in enumerate((mine, theirs)):
            row = ((core ^ other) * chips + (chip ^ k)) * share
            slopes[pl.ds(pl.multiple_of(row, share), share), :] = pieces[k][...]
    for k in range(kept):
        total = (keep[k] + got[k].astype(F32)).astype(BF16)
        for p in range(2):
            for r in range(levels):
                at, column = (k * levels + r) * part, (p * levels + r) * rows
                turned[at:at + part, p * rows:(p + 1) * rows] = total[:, column:column + rows]
    terms = jnp.dot(turned[...], slopes[...], preferred_element_type=F32)
    users = chunks.shape[0]
    groups = part // few
    for u in range(users):
        for block in range(kept * levels):
            first = block * part + (u % groups) * few
            column = (u // groups) * LANES
            chunks[u, block * few:(block + 1) * few] = terms[first:first + few, column:column + LANES]

    _, tile, width = items.shape
    item_few = tile // users
    for k, out in enumerate(outs):
        first = pl.multiple_of((user ^ k) * item_few, item_few)
        blocks = [
            items[z, pl.ds(first, item_few), column:column + LANES]
            for column in range(0, width, LANES)
            for z in range(chips)
        ]
        fill(out, *blocks, chunks[user ^ k])


def fill(out, *blocks):
    at = 0
    for block in blocks:
        out[at:at + block.shape[0]] = block.astype(out.dtype)
        at += block.shape[0]
    if at < out.shape[0]:
        out[at:] = jnp.zeros((out.shape[0] - at,) + out.shape[1:], out.dtype)


def user_sum(chips, few, blocks, rows, *refs):
    count = len(refs) - chips - 1
    parts, outs, total = refs[:count], refs[count:-1], refs[-1]
    chip, _ = here()
    summed = parts[0][...]
    for part in parts[1:]:
        summed = summed + part[...].astype(F32)
    for block in range(blocks):
        for z in range(chips):
            at = (block * chips + z) * few
            total[z, block * few:(block + 1) * few] = summed[at:at + few]
    first = blocks * chips * few
    weight = summed[first:first + rows].astype(BF16)
    for k, out in enumerate(outs):
        fill(out, total[chip ^ k], weight)


def line_sum(items, rows, stride, own, *refs):
    *parts, out = refs
    made = dict(zip(reach(len(parts)), parts))
    parts = [own] + [made[k] for k in sorted(made)]
    total = own[:items]
    for part in parts[1:]:
        total = total + part[:items].astype(F32)
    blocks = [total]
    for k in range(len(parts)):
        terms = []
        for j in range(k % stride, len(parts), stride):
            at = items + ((j ^ k) // stride) * rows
            terms.append(parts[j][at:at + rows].astype(BF16).astype(F32))
        blocks.append(tree_sum(terms))
    fill(out, *blocks)


def weight_out(chips, items, few, scale, counts, *refs):
    users, places = counts
    pieces = refs[:users + len(places)]
    out, wide, loose, item_rows, sems = refs[-5:]
    chip, core = here()
    user = lax.axis_index("user")
    _, levels, half, hidden = wide.shape
    part = half // chips
    groups = part // few
    copies = []

    def send(source, target):
        copies.append(pltpu.make_async_copy(source, target, sems.at[len(copies)]))
        copies[-1].start()

    def rows_of(piece, k, r):
        at = items + (k * levels + r) * few
        return piece[at:at + few].astype(F32) * scale

    if users:
        item_few = item_rows.shape[0] // users
        for j in range(users):
            row = pl.multiple_of((user ^ j) * item_few, item_few)
            for block in range(items // item_few):
                item_rows[pl.ds(row, item_few), block * LANES:(block + 1) * LANES] = (
                    pieces[j][block * item_few:(block + 1) * item_few].astype(F32)
                )
        send(item_rows, refs[-6])
    for other, js in ((0, range(users)), (1, places)):
        first = pl.multiple_of((core ^ other) * half, half)
        base = users if other else 0
        for r in range(levels):
            for at, j in enumerate(js):
                column = pl.multiple_of((user ^ j) // groups * LANES, LANES)
                for k in range(chips):
                    block = rows_of(pieces[base + at], k, r)
                    if groups == 1:
                        row = pl.multiple_of((chip ^ k) * part, part)
                        wide[other, r, pl.ds(row, part), pl.ds(column, LANES)] = block
                    else:
                        loose[chip ^ k, user ^ j] = block
                if groups == 1 and other:
                    send(wide.at[other, r, :, pl.ds(column, LANES)],
                         out.at[r, pl.ds(first, half), pl.ds(column, LANES)])
            if groups > 1 and len(js):
                for z in range(chips):
                    for u in range(len(js)):
                        row, column = z * part + (u % groups) * few, (u // groups) * LANES
                        wide[other, r, row:row + few, column:column + LANES] = loose[z, u]
            if len(js) and (groups > 1 or not other):
                send(wide.at[other, r], out.at[r, pl.ds(first, half), :])
    for copy in copies:
        copy.wait()


def per_device(item_features, level_weights, tile_values, tile_order, tile_counts, cotangent):
    item_size = lax.axis_size("item")
    user_size = lax.axis_size("user")
    chips = item_size // 2
    levels, width, hidden_width = level_weights.shape
    tile = tile_values.shape[-1]
    capacity = tile_values.shape[2]
    items = item_features.shape[0] * item_size
    block_count = items // tile
    user_blocks = tile_order.shape[1] // (levels * block_count)
    group_rows = user_blocks * tile
    share = group_rows // item_size
    rows = levels * chips * share
    vmem, anywhere = space(pltpu.VMEM), space(pl.ANY)

    strips = tile // (2 * share)
    tiles = tile_values.reshape(1, capacity, strips, 2, share, tile)
    other_tiles = swap(tiles, "item", 1)
    far = swap_each([item_features] * (chips - 1), "item", 2)
    dense = call(
        functools.partial(place_tiles, block_count),
        struct((2, rows, items), BF16),
        (tile_order, tile_counts, tiles, other_tiles),
        4,
        scratch=[
            pltpu.SMEM(tile_order.shape, jnp.int32),
            pltpu.SMEM(tile_counts.shape, jnp.int32),
            pltpu.SemaphoreType.DMA((2 * capacity * strips + 2,)),
        ],
        specs=[space(pltpu.HBM)] * 3 + [anywhere],
    )
    far, dense = together(far, dense)
    mine = [item_features, *far]
    theirs = [swap(piece, "item", 1) for piece in mine]
    half_features = struct((items // 2, width), BF16)
    my_features, aggregate = call(
        forward_mine,
        (half_features, struct((rows, width), F32)),
        (dense, *mine),
        0.7,
    )
    piece = struct((share, hidden_width), BF16)
    their_features, pre_own, *pre_sends = call(
        functools.partial(forward_theirs, chips),
        (half_features, struct((share, hidden_width), F32)) + (piece,) * (chips - 1),
        (dense, level_weights, *theirs, aggregate),
        1,
        scratch=[pltpu.VMEM((chips, share, hidden_width), F32)],
    )
    pre_parts = swap_each(pre_sends, "item", 2)

    part = width // item_size
    kept = chips // 2
    turned_own, turned_send = call(
        functools.partial(turn, levels),
        (struct((kept, part, 2 * rows), F32), struct((kept, part, 2 * rows), BF16)),
        (dense, my_features, their_features),
        3,
        scratch=[pltpu.VMEM((chips, part, 2 * rows), F32)],
    )
    turned_got = swap(turned_send, "item", 2)

    flipped, weights_t = call(
        flip,
        (struct((2, items // 2, rows), BF16), struct((levels, hidden_width, width), BF16)),
        (dense, level_weights),
        1.5,
    )
    *pre_parts, flipped, weights_t = lax.optimization_barrier(
        (*by_reach(pre_parts), flipped, weights_t)
    )
    pre, slope = call(
        slopes_of,
        (struct((share, hidden_width), F32), piece),
        (pre_own, *pre_parts, cotangent),
        0.1,
    )
    far = swap_each([slope] * (chips - 1), "item", 2)
    hidden = call(activate, piece, (pre,), 0.7)
    mine = [slope, *far]
    theirs = [swap(piece, "item", 1) for piece in mine]
    *theirs, turned_got = lax.optimization_barrier((*theirs, turned_got))

    item_part = call(
        backward_mine,
        struct((chips, tile, width), F32),
        (flipped, weights_t, *mine),
        1,
        scratch=[
            pltpu.VMEM((chips * share, hidden_width), BF16), pltpu.VMEM((rows, width), BF16)
        ],
    )

    def padded(amount):
        return -(-amount // 16) * 16

    few = part * min(hidden_width // LANES, user_size) // user_size
    item_few = tile // user_size
    blocks = width // LANES
    count = kept * levels * few
    amount = padded(blocks * chips * item_few + count)
    own, *sends = call(
        functools.partial(backward_theirs, chips, few),
        (struct((amount, LANES), F32),) + (struct((amount, LANES), BF16),) * (user_size - 1),
        (flipped, weights_t, *mine, *theirs, item_part, turned_own, turned_got),
        1.3,
        scratch=[
            pltpu.VMEM((chips * share, hidden_width), BF16),
            pltpu.VMEM((rows, width), BF16),
            pltpu.VMEM((chips, tile, width), F32),
            pltpu.VMEM((kept * levels * part, group_rows), BF16),
            pltpu.VMEM((group_rows, hidden_width), BF16),
            pltpu.VMEM((user_size, count, LANES), F32),
        ],
    )
    parts = swap_each(sends, "user", 1)
    parts, hidden = together(parts, hidden)
    amount = padded(blocks * item_few + count)
    own, *sends = call(
        functools.partial(user_sum, chips, item_few, blocks, count),
        (struct((amount, LANES), F32),) + (struct((amount, LANES), BF16),) * (chips - 1),
        (own, *parts[::-1]),
        0.1,
        scratch=[pltpu.VMEM((chips, blocks * item_few, LANES), F32)],
    )
    parts = swap_each(sends, "item", 2)
    amount = padded(blocks * item_few + chips * levels * few)
    gathered = call(
        functools.partial(line_sum, blocks * item_few, levels * few, chips // kept),
        struct((amount, LANES), BF16),
        (own, *by_reach(parts)),
        0.1,
    )
    gathered = [gathered] + swap_each([gathered] * (user_size - 1), "user", 1)
    others = [swap(piece, "item", 1) for piece in gathered]
    weight_grad = struct((levels, width, hidden_width), F32)
    late = list(range(user_size))
    soon = [late.pop(0), late.pop()] if few == part else []
    scratch = [
        pltpu.VMEM((2, levels, width // 2, hidden_width), F32),
        pltpu.VMEM((chips, user_size, few, LANES), F32),
        pltpu.VMEM((tile, width), F32),
        pltpu.SemaphoreType.DMA((levels * (user_size + 1) + 1,)),
    ]
    put = functools.partial(
        weight_out, chips, blocks * item_few, few, (group_rows * user_size) ** -0.5
    )
    item_grad, half_grad = call(
        functools.partial(put, (user_size, soon)),
        (struct((tile, width), F32), weight_grad),
        (*gathered, *[others[j] for j in soon]),
        0.9,
        scratch=scratch,
        out_specs=(anywhere, anywhere),
    )
    weight_grad = call(
        functools.partial(put, (0, late)),
        weight_grad,
        (*[others[j] for j in late], half_grad),
        0.9,
        scratch=scratch,
        specs=[vmem] * len(late) + [anywhere],
        out_specs=anywhere,
        aliases={len(late): 0},
    )
    return hidden, item_grad, weight_grad


def solution(mesh):
    in_specs = (
        P("item", None),
        P(),
        P("user", "item", None, None, None),
        P("user", None),
        P("user", None),
        P(("user", "item"), None),
    )
    out_specs = (P(("user", "item"), None), P("item", None), P())
    return jax.shard_map(
        per_device, mesh=mesh, in_specs=in_specs, out_specs=out_specs, check_vma=False
    )
```

```python
import functools
import jax
import jax.numpy as jnp
from jax import lax
from jax.experimental import pallas as pl
from jax.experimental.pallas import tpu as pltpu
from jax.sharding import PartitionSpec as P

BF16 = jnp.bfloat16
F32 = jnp.float32
VMEM_LIMIT = 24 * 1024 * 1024
LANES = 128


def swap(array, axis, step):
    return lax.ppermute(array, axis, [(i, i ^ step) for i in range(lax.axis_size(axis))])


def swap_each(arrays, axis, unit):
    return [swap(array, axis, (k + 1) * unit) for k, array in enumerate(arrays)]


def reach(count):
    return sorted(range(1, count + 1), key=lambda k: (-k.bit_length(), k))


def by_reach(parts):
    return [parts[k - 1] for k in reach(len(parts))]


def together(parts, *others):
    out = lax.optimization_barrier((*parts, *others))
    return list(out[:len(parts)]), *out[len(parts):]


def tree_sum(parts):
    while len(parts) > 1:
        parts = [parts[i] + parts[i + 1] for i in range(0, len(parts), 2)]
    return parts[0]


def cost(microseconds):
    return pl.CostEstimate(
        flops=int(microseconds * 1e9), bytes_accessed=int(microseconds * 3e6), transcendentals=0
    )


def struct(shape, dtype):
    return jax.ShapeDtypeStruct(shape, dtype)


def space(memory_space):
    return pl.BlockSpec(memory_space=memory_space)


def call(body, outs, args, time, scratch=(), specs=None, out_specs=None, aliases=None):
    vmem = space(pltpu.VMEM)
    return pl.pallas_call(
        body,
        out_shape=outs,
        in_specs=specs or [vmem] * len(args),
        out_specs=out_specs or jax.tree.map(lambda _: vmem, outs),
        scratch_shapes=list(scratch),
        compiler_params=pltpu.CompilerParams(vmem_limit_bytes=VMEM_LIMIT),
        cost_estimate=cost(time),
        input_output_aliases=aliases or {},
    )(*args)


def hbm(array):
    return pltpu.with_memory_space_constraint(array, pltpu.HBM)


def here():
    item = lax.axis_index("item")
    return item // 2, item % 2


def place_tiles(block_count, order, counts, mine, theirs, dense, order_s, counts_s, sems):
    tile = mine.shape[-1]
    capacity, strips, _, share = mine.shape[1:5]
    chips = counts.shape[1] // 2
    user_blocks = chips // strips
    scalars = [
        pltpu.make_async_copy(order, order_s, sems.at[2 * capacity * strips]),
        pltpu.make_async_copy(counts, counts_s, sems.at[2 * capacity * strips + 1]),
    ]
    for scalar in scalars:
        scalar.start()
    dense[...] = jnp.zeros_like(dense)
    for scalar in scalars:
        scalar.wait()
    copies = []
    for other, tiles in enumerate((mine, theirs)):
        cell = lax.axis_index("item") ^ other
        before = jnp.int32(0)
        for c in range(counts.shape[1]):
            before = before + jnp.where(c < cell, counts_s[0, c], 0)
        holding = counts_s[0, cell]
        for t in range(capacity):
            copies.append((other * capacity + t, tiles, t, before, holding))

    def copy(number, tiles, t, before, strip):
        slot = order_s[0, jnp.minimum(before + t, order.shape[1] - 1)]
        target, block = slot // block_count, slot % block_count
        level, user_block = target // user_blocks, target % user_blocks
        row = (level * chips + user_block * strips + strip) * share
        column = ((block % 2) * chips + block // 2) * tile
        return pltpu.make_async_copy(
            tiles.at[0, t, strip],
            dense.at[:, pl.ds(pl.multiple_of(row, share), share),
                     pl.ds(pl.multiple_of(column, tile), tile)],
            sems.at[number * strips + strip],
        )

    for number, tiles, t, before, holding in copies:
        @pl.when(t < holding)
        def _():
            for strip in range(strips):
                copy(number, tiles, t, before, strip).start()
    for number, tiles, t, before, holding in copies:
        @pl.when(t < holding)
        def _():
            for strip in range(strips):
                copy(number, tiles, t, before, strip).wait()


def stack(pieces, out):
    chip, _ = here()
    size = pieces[0].shape[0]
    for k, piece in enumerate(pieces):
        out[pl.ds(pl.multiple_of((chip ^ k) * size, size), size), :] = piece[...]


def columns_of(dense, parity):
    half = dense.shape[2] // 2
    return pl.ds(pl.multiple_of(parity * half, half), half)


def forward_mine(dense, *refs):
    *pieces, features, terms = refs
    _, core = here()
    stack(pieces, features)
    terms[...] = jnp.dot(
        dense[core, :, columns_of(dense, core)], features[...], preferred_element_type=F32
    )


def forward_theirs(chips, dense, weights, *refs):
    pieces = refs[:chips]
    before, features, own, *sends, pre = refs[chips:]
    chip, core = here()
    levels, _, hidden = weights.shape
    stack(pieces, features)
    rows = dense.shape[1] // levels
    total = jnp.zeros((rows, hidden), F32)
    for r in range(levels):
        at = pl.ds(r * rows, rows)
        block = before[at, :] + jnp.dot(
            dense[core, at, columns_of(dense, 1 - core)], features[...], preferred_element_type=F32
        )
        total = total + jnp.dot(block.astype(BF16), weights[r], preferred_element_type=F32)
    pre[...] = total.reshape(pre.shape)
    own[...] = pre[chip]
    for k in range(1, chips):
        sends[k - 1][...] = pre[chip ^ k].astype(BF16)


def turn(levels, dense, mine, theirs, own, send, turned):
    chip, core = here()
    chips, part, _ = turned.shape
    half = chips * part
    rows = dense.shape[1] // levels
    width = pl.ds(pl.multiple_of(core * half, half), half)
    for p in range(2):
        for r in range(levels):
            at = p * levels * rows + r * rows
            block = jnp.zeros((rows, half), F32)
            for parity, features in ((core, mine), (1 - core, theirs)):
                block = block + jnp.dot(
                    dense[p, pl.ds(r * rows, rows), columns_of(dense, parity)],
                    features[:, width],
                    preferred_element_type=F32,
                )
            turned[:, :, at:at + rows] = block.T.reshape(chips, part, rows)
    for k in range(0, chips, 2):
        own[k // 2] = turned[chip ^ k]
        send[k // 2] = turned[chip ^ (k + 1)].astype(BF16)


def flip(dense, weights, flipped, weights_t):
    _, core = here()
    step = dense.shape[1] // weights.shape[0]
    for r in range(weights.shape[0]):
        weights_t[r] = weights[r].T
        for p in range(2):
            at = pl.ds(r * step, step)
            flipped[p, :, at] = dense[p, at, columns_of(dense, core)].T


def slopes_of(own, *refs):
    *parts, cotangent, pre_out, slope = refs
    pre = own[...]
    for part in parts:
        pre = pre + part[...].astype(F32)
    sigmoid = 1.0 / (1.0 + jnp.exp(-pre))
    pre_out[...] = pre
    slope[...] = (cotangent[...].astype(F32) * (sigmoid * (1.0 + pre * (1.0 - sigmoid)))).astype(BF16)


def activate(pre, hidden):
    hidden[...] = (pre[...] / (1.0 + jnp.exp(-pre[...]))).astype(BF16)


def item_terms(other, flipped, weights_t, pieces, slopes, back):
    _, core = here()
    stack(pieces, slopes)
    rows = slopes.shape[0]
    for r in range(weights_t.shape[0]):
        back[r * rows:(r + 1) * rows, :] = jnp.dot(
            slopes[...], weights_t[r], preferred_element_type=F32
        ).astype(BF16)
    return jnp.dot(flipped[core ^ other], back[...], preferred_element_type=F32)


def backward_mine(flipped, weights_t, *refs):
    *pieces, out, slopes, back = refs
    out[...] = item_terms(0, flipped, weights_t, pieces, slopes, back).reshape(out.shape)


def backward_theirs(chips, few, flipped, weights_t, *refs):
    mine, theirs = refs[:chips], refs[chips:2 * chips]
    before, keep, got, *outs, their_slopes, back, items, turned, slopes, chunks = refs[2 * chips:]
    chip, core = here()
    user = lax.axis_index("user")
    levels = weights_t.shape[0]
    terms = item_terms(1, flipped, weights_t, theirs, their_slopes, back)
    items[...] = before[...] + terms.reshape(items.shape)

    share = mine[0].shape[0]
    kept, part, columns = keep.shape
    rows = columns // (2 * levels)
    for k in range(chips):
        for other, pieces in enumerate((mine, theirs)):
            row = ((core ^ other) * chips + (chip ^ k)) * share
            slopes[pl.ds(pl.multiple_of(row, share), share), :] = pieces[k][...]
    for k in range(kept):
        total = (keep[k] + got[k].astype(F32)).astype(BF16)
        for p in range(2):
            for r in range(levels):
                at, column = (k * levels + r) * part, (p * levels + r) * rows
                turned[at:at + part, p * rows:(p + 1) * rows] = total[:, column:column + rows]
    terms = jnp.dot(turned[...], slopes[...], preferred_element_type=F32)
    users = chunks.shape[0]
    groups = part // few
    for u in range(users):
        for block in range(kept * levels):
            first = block * part + (u % groups) * few
            column = (u // groups) * LANES
            chunks[u, block * few:(block + 1) * few] = terms[first:first + few, column:column + LANES]

    _, tile, width = items.shape
    item_few = tile // users
    for k, out in enumerate(outs):
        first = pl.multiple_of((user ^ k) * item_few, item_few)
        blocks = [
            items[z, pl.ds(first, item_few), column:column + LANES]
            for column in range(0, width, LANES)
            for z in range(chips)
        ]
        fill(out, *blocks, chunks[user ^ k])


def fill(out, *blocks):
    at = 0
    for block in blocks:
        out[at:at + block.shape[0]] = block.astype(out.dtype)
        at += block.shape[0]
    if at < out.shape[0]:
        out[at:] = jnp.zeros((out.shape[0] - at,) + out.shape[1:], out.dtype)


def user_sum(chips, few, blocks, rows, *refs):
    count = len(refs) - chips - 1
    parts, outs, total = refs[:count], refs[count:-1], refs[-1]
    chip, _ = here()
    summed = parts[0][...]
    for part in parts[1:]:
        summed = summed + part[...].astype(F32)
    for block in range(blocks):
        for z in range(chips):
            at = (block * chips + z) * few
            total[z, block * few:(block + 1) * few] = summed[at:at + few]
    first = blocks * chips * few
    weight = summed[first:first + rows].astype(BF16)
    for k, out in enumerate(outs):
        fill(out, total[chip ^ k], weight)


def line_sum(items, rows, stride, own, *refs):
    *parts, out = refs
    made = dict(zip(reach(len(parts)), parts))
    parts = [own] + [made[k] for k in sorted(made)]
    total = own[:items]
    for part in parts[1:]:
        total = total + part[:items].astype(F32)
    blocks = [total]
    for k in range(len(parts)):
        terms = []
        for j in range(k % stride, len(parts), stride):
            at = items + ((j ^ k) // stride) * rows
            terms.append(parts[j][at:at + rows].astype(BF16).astype(F32))
        blocks.append(tree_sum(terms))
    fill(out, *blocks)


def weight_out(chips, items, few, scale, counts, *refs):
    users, places = counts
    pieces = refs[:users + len(places)]
    out, wide, loose, item_rows, sems = refs[-5:]
    chip, core = here()
    user = lax.axis_index("user")
    _, levels, half, hidden = wide.shape
    part = half // chips
    groups = part // few
    copies = []

    def send(source, target):
        copies.append(pltpu.make_async_copy(source, target, sems.at[len(copies)]))
        copies[-1].start()

    def rows_of(piece, k, r):
        at = items + (k * levels + r) * few
        return piece[at:at + few].astype(F32) * scale

    if users:
        item_few = item_rows.shape[0] // users
        for j in range(users):
            row = pl.multiple_of((user ^ j) * item_few, item_few)
            for block in range(items // item_few):
                item_rows[pl.ds(row, item_few), block * LANES:(block + 1) * LANES] = (
                    pieces[j][block * item_few:(block + 1) * item_few].astype(F32)
                )
        send(item_rows, refs[-6])
    for other, js in ((0, range(users)), (1, places)):
        first = pl.multiple_of((core ^ other) * half, half)
        base = users if other else 0
        for r in range(levels):
            for at, j in enumerate(js):
                column = pl.multiple_of((user ^ j) // groups * LANES, LANES)
                for k in range(chips):
                    block = rows_of(pieces[base + at], k, r)
                    if groups == 1:
                        row = pl.multiple_of((chip ^ k) * part, part)
                        wide[other, r, pl.ds(row, part), pl.ds(column, LANES)] = block
                    else:
                        loose[chip ^ k, user ^ j] = block
                if groups == 1 and other:
                    send(wide.at[other, r, :, pl.ds(column, LANES)],
                         out.at[r, pl.ds(first, half), pl.ds(column, LANES)])
            if groups > 1 and len(js):
                for z in range(chips):
                    for u in range(len(js)):
                        row, column = z * part + (u % groups) * few, (u // groups) * LANES
                        wide[other, r, row:row + few, column:column + LANES] = loose[z, u]
            if len(js) and (groups > 1 or not other):
                send(wide.at[other, r], out.at[r, pl.ds(first, half), :])
    for copy in copies:
        copy.wait()


def per_device(item_features, level_weights, tile_values, tile_order, tile_counts, cotangent):
    item_size = lax.axis_size("item")
    user_size = lax.axis_size("user")
    chips = item_size // 2
    levels, width, hidden_width = level_weights.shape
    tile = tile_values.shape[-1]
    capacity = tile_values.shape[2]
    items = item_features.shape[0] * item_size
    block_count = items // tile
    user_blocks = tile_order.shape[1] // (levels * block_count)
    group_rows = user_blocks * tile
    share = group_rows // item_size
    rows = levels * chips * share
    vmem, anywhere = space(pltpu.VMEM), space(pl.ANY)

    strips = tile // (2 * share)
    tiles = tile_values.reshape(1, capacity, strips, 2, share, tile)
    other_tiles = swap(tiles, "item", 1)
    far = swap_each([item_features] * (chips - 1), "item", 2)
    dense = call(
        functools.partial(place_tiles, block_count),
        struct((2, rows, items), BF16),
        (hbm(tile_order), hbm(tile_counts), hbm(tiles), other_tiles),
        4,
        scratch=[
            pltpu.SMEM(tile_order.shape, jnp.int32),
            pltpu.SMEM(tile_counts.shape, jnp.int32),
            pltpu.SemaphoreType.DMA((2 * capacity * strips + 2,)),
        ],
        specs=[space(pltpu.HBM)] * 3 + [anywhere],
    )
    far, dense = together(far, dense)
    mine = [item_features, *far]
    theirs = [swap(piece, "item", 1) for piece in mine]
    half_features = struct((items // 2, width), BF16)
    my_features, aggregate = call(
        forward_mine,
        (half_features, struct((rows, width), F32)),
        (dense, *mine),
        0.7,
    )
    piece = struct((share, hidden_width), BF16)
    their_features, pre_own, *pre_sends = call(
        functools.partial(forward_theirs, chips),
        (half_features, struct((share, hidden_width), F32)) + (piece,) * (chips - 1),
        (dense, level_weights, *theirs, aggregate),
        1,
        scratch=[pltpu.VMEM((chips, share, hidden_width), F32)],
    )
    pre_parts = swap_each(pre_sends, "item", 2)

    part = width // item_size
    kept = chips // 2
    turned_own, turned_send = call(
        functools.partial(turn, levels),
        (struct((kept, part, 2 * rows), F32), struct((kept, part, 2 * rows), BF16)),
        (dense, my_features, their_features),
        3,
        scratch=[pltpu.VMEM((chips, part, 2 * rows), F32)],
    )
    turned_got = swap(turned_send, "item", 2)

    flipped, weights_t = call(
        flip,
        (struct((2, items // 2, rows), BF16), struct((levels, hidden_width, width), BF16)),
        (dense, level_weights),
        1.5,
    )
    *pre_parts, flipped, weights_t = lax.optimization_barrier(
        (*by_reach(pre_parts), flipped, weights_t)
    )
    pre, slope = call(
        slopes_of,
        (struct((share, hidden_width), F32), piece),
        (pre_own, *pre_parts, cotangent),
        0.1,
    )
    far = swap_each([slope] * (chips - 1), "item", 2)
    hidden = call(activate, piece, (pre,), 0.7)
    mine = [slope, *far]
    theirs = [swap(piece, "item", 1) for piece in mine]
    *theirs, turned_got = lax.optimization_barrier((*theirs, turned_got))

    item_part = call(
        backward_mine,
        struct((chips, tile, width), F32),
        (flipped, weights_t, *mine),
        1,
        scratch=[
            pltpu.VMEM((chips * share, hidden_width), BF16), pltpu.VMEM((rows, width), BF16)
        ],
    )

    def padded(amount):
        return -(-amount // 16) * 16

    few = part * min(hidden_width // LANES, user_size) // user_size
    item_few = tile // user_size
    blocks = width // LANES
    count = kept * levels * few
    amount = padded(blocks * chips * item_few + count)
    own, *sends = call(
        functools.partial(backward_theirs, chips, few),
        (struct((amount, LANES), F32),) + (struct((amount, LANES), BF16),) * (user_size - 1),
        (flipped, weights_t, *mine, *theirs, item_part, turned_own, turned_got),
        1.3,
        scratch=[
            pltpu.VMEM((chips * share, hidden_width), BF16),
            pltpu.VMEM((rows, width), BF16),
            pltpu.VMEM((chips, tile, width), F32),
            pltpu.VMEM((kept * levels * part, group_rows), BF16),
            pltpu.VMEM((group_rows, hidden_width), BF16),
            pltpu.VMEM((user_size, count, LANES), F32),
        ],
    )
    parts = swap_each(sends, "user", 1)
    parts, hidden = together(parts, hidden)
    amount = padded(blocks * item_few + count)
    own, *sends = call(
        functools.partial(user_sum, chips, item_few, blocks, count),
        (struct((amount, LANES), F32),) + (struct((amount, LANES), BF16),) * (chips - 1),
        (own, *parts[::-1]),
        0.1,
        scratch=[pltpu.VMEM((chips, blocks * item_few, LANES), F32)],
    )
    parts = swap_each(sends, "item", 2)
    amount = padded(blocks * item_few + chips * levels * few)
    gathered = call(
        functools.partial(line_sum, blocks * item_few, levels * few, chips // kept),
        struct((amount, LANES), BF16),
        (own, *by_reach(parts)),
        0.1,
    )
    gathered = [gathered] + swap_each([gathered] * (user_size - 1), "user", 1)
    others = [swap(piece, "item", 1) for piece in gathered]
    weight_grad = struct((levels, width, hidden_width), F32)
    late = list(range(user_size))
    soon = [late.pop(0), late.pop()] if few == part else []
    scratch = [
        pltpu.VMEM((2, levels, width // 2, hidden_width), F32),
        pltpu.VMEM((chips, user_size, few, LANES), F32),
        pltpu.VMEM((tile, width), F32),
        pltpu.SemaphoreType.DMA((levels * (user_size + 1) + 1,)),
    ]
    put = functools.partial(
        weight_out, chips, blocks * item_few, few, (group_rows * user_size) ** -0.5
    )
    item_grad, half_grad = call(
        functools.partial(put, (user_size, soon)),
        (struct((tile, width), F32), weight_grad),
        (*gathered, *[others[j] for j in soon]),
        0.9,
        scratch=scratch,
        out_specs=(anywhere, anywhere),
    )
    weight_grad = call(
        functools.partial(put, (0, late)),
        weight_grad,
        (*[others[j] for j in late], half_grad),
        0.9,
        scratch=scratch,
        specs=[vmem] * len(late) + [anywhere],
        out_specs=anywhere,
        aliases={len(late): 0},
    )
    return hidden, item_grad, weight_grad


def solution(mesh):
    in_specs = (
        P("item", None),
        P(),
        P("user", "item", None, None, None),
        P("user", None),
        P("user", None),
        P(("user", "item"), None),
    )
    out_specs = (P(("user", "item"), None), P("item", None), P())
    return jax.shard_map(
        per_device, mesh=mesh, in_specs=in_specs, out_specs=out_specs, check_vma=False
    )
```

```python
import functools
import jax
import jax.numpy as jnp
from jax import lax
from jax.experimental import pallas as pl
from jax.experimental.pallas import tpu as pltpu
from jax.sharding import PartitionSpec as P

BF16 = jnp.bfloat16
F32 = jnp.float32
VMEM_LIMIT = 24 * 1024 * 1024
LANES = 128


def swap(array, axis, step):
    return lax.ppermute(array, axis, [(i, i ^ step) for i in range(lax.axis_size(axis))])


def swap_each(arrays, axis, unit):
    return [swap(array, axis, (k + 1) * unit) for k, array in enumerate(arrays)]


def reach(count):
    return sorted(range(1, count + 1), key=lambda k: (-k.bit_length(), k))


def by_reach(parts):
    return [parts[k - 1] for k in reach(len(parts))]


def together(parts, *others):
    out = lax.optimization_barrier((*parts, *others))
    return list(out[:len(parts)]), *out[len(parts):]


def tree_sum(parts):
    while len(parts) > 1:
        parts = [parts[i] + parts[i + 1] for i in range(0, len(parts), 2)]
    return parts[0]


def cost(microseconds):
    return pl.CostEstimate(
        flops=int(microseconds * 1e9), bytes_accessed=int(microseconds * 3e6), transcendentals=0
    )


def struct(shape, dtype):
    return jax.ShapeDtypeStruct(shape, dtype)


def space(memory_space):
    return pl.BlockSpec(memory_space=memory_space)


def call(body, outs, args, time, scratch=(), specs=None, out_specs=None, aliases=None):
    vmem = space(pltpu.VMEM)
    return pl.pallas_call(
        body,
        out_shape=outs,
        in_specs=specs or [vmem] * len(args),
        out_specs=out_specs or jax.tree.map(lambda _: vmem, outs),
        scratch_shapes=list(scratch),
        compiler_params=pltpu.CompilerParams(vmem_limit_bytes=VMEM_LIMIT),
        cost_estimate=cost(time),
        input_output_aliases=aliases or {},
    )(*args)


def hbm(array):
    return pltpu.with_memory_space_constraint(array, pltpu.HBM)


def here():
    item = lax.axis_index("item")
    return item // 2, item % 2


def place_tiles(block_count, order, counts, mine, theirs, dense, order_s, counts_s, sems):
    tile = mine.shape[-1]
    capacity, strips, _, share = mine.shape[1:5]
    chips = counts.shape[1] // 2
    user_blocks = chips // strips
    scalars = [
        pltpu.make_async_copy(order, order_s, sems.at[2 * capacity * strips]),
        pltpu.make_async_copy(counts, counts_s, sems.at[2 * capacity * strips + 1]),
    ]
    for scalar in scalars:
        scalar.start()
    dense[...] = jnp.zeros_like(dense)
    for scalar in scalars:
        scalar.wait()
    copies = []
    for other, tiles in enumerate((mine, theirs)):
        cell = lax.axis_index("item") ^ other
        before = jnp.int32(0)
        for c in range(counts.shape[1]):
            before = before + jnp.where(c < cell, counts_s[0, c], 0)
        holding = counts_s[0, cell]
        for t in range(capacity):
            copies.append((other * capacity + t, tiles, t, before, holding))

    def copy(number, tiles, t, before, strip):
        slot = order_s[0, jnp.minimum(before + t, order.shape[1] - 1)]
        target, block = slot // block_count, slot % block_count
        level, user_block = target // user_blocks, target % user_blocks
        row = (level * chips + user_block * strips + strip) * share
        column = ((block % 2) * chips + block // 2) * tile
        return pltpu.make_async_copy(
            tiles.at[0, t, strip],
            dense.at[:, pl.ds(pl.multiple_of(row, share), share),
                     pl.ds(pl.multiple_of(column, tile), tile)],
            sems.at[number * strips + strip],
        )

    for number, tiles, t, before, holding in copies:
        @pl.when(t < holding)
        def _():
            for strip in range(strips):
                copy(number, tiles, t, before, strip).start()
    for number, tiles, t, before, holding in copies:
        @pl.when(t < holding)
        def _():
            for strip in range(strips):
                copy(number, tiles, t, before, strip).wait()


def stack(pieces, out):
    chip, _ = here()
    size = pieces[0].shape[0]
    for k, piece in enumerate(pieces):
        out[pl.ds(pl.multiple_of((chip ^ k) * size, size), size), :] = piece[...]


def columns_of(dense, parity):
    half = dense.shape[2] // 2
    return pl.ds(pl.multiple_of(parity * half, half), half)


def forward_mine(dense, *refs):
    *pieces, features, terms = refs
    _, core = here()
    stack(pieces, features)
    terms[...] = jnp.dot(
        dense[core, :, columns_of(dense, core)], features[...], preferred_element_type=F32
    )


def forward_theirs(chips, dense, weights, *refs):
    pieces = refs[:chips]
    before, features, own, *sends, pre = refs[chips:]
    chip, core = here()
    levels, _, hidden = weights.shape
    stack(pieces, features)
    rows = dense.shape[1] // levels
    total = jnp.zeros((rows, hidden), F32)
    for r in range(levels):
        at = pl.ds(r * rows, rows)
        block = before[at, :] + jnp.dot(
            dense[core, at, columns_of(dense, 1 - core)], features[...], preferred_element_type=F32
        )
        total = total + jnp.dot(block.astype(BF16), weights[r], preferred_element_type=F32)
    pre[...] = total.reshape(pre.shape)
    own[...] = pre[chip]
    for k in range(1, chips):
        sends[k - 1][...] = pre[chip ^ k].astype(BF16)


def turn(levels, dense, mine, theirs, own, send, turned):
    chip, core = here()
    chips, part, _ = turned.shape
    half = chips * part
    rows = dense.shape[1] // levels
    width = pl.ds(pl.multiple_of(core * half, half), half)
    for p in range(2):
        for r in range(levels):
            at = p * levels * rows + r * rows
            block = jnp.zeros((rows, half), F32)
            for parity, features in ((core, mine), (1 - core, theirs)):
                block = block + jnp.dot(
                    dense[p, pl.ds(r * rows, rows), columns_of(dense, parity)],
                    features[:, width],
                    preferred_element_type=F32,
                )
            turned[:, :, at:at + rows] = block.T.reshape(chips, part, rows)
    for k in range(0, chips, 2):
        own[k // 2] = turned[chip ^ k]
        send[k // 2] = turned[chip ^ (k + 1)].astype(BF16)


def flip(dense, weights, flipped, weights_t):
    _, core = here()
    step = dense.shape[1] // weights.shape[0]
    for r in range(weights.shape[0]):
        weights_t[r] = weights[r].T
        for p in range(2):
            at = pl.ds(r * step, step)
            flipped[p, :, at] = dense[p, at, columns_of(dense, core)].T


def slopes_of(own, *refs):
    *parts, cotangent, pre_out, slope = refs
    pre = own[...]
    for part in parts:
        pre = pre + part[...].astype(F32)
    sigmoid = 1.0 / (1.0 + jnp.exp(-pre))
    pre_out[...] = pre
    slope[...] = (cotangent[...].astype(F32) * (sigmoid * (1.0 + pre * (1.0 - sigmoid)))).astype(BF16)


def activate(pre, hidden):
    hidden[...] = (pre[...] / (1.0 + jnp.exp(-pre[...]))).astype(BF16)


def item_terms(other, flipped, weights_t, pieces, slopes, back):
    _, core = here()
    stack(pieces, slopes)
    rows = slopes.shape[0]
    for r in range(weights_t.shape[0]):
        back[r * rows:(r + 1) * rows, :] = jnp.dot(
            slopes[...], weights_t[r], preferred_element_type=F32
        ).astype(BF16)
    return jnp.dot(flipped[core ^ other], back[...], preferred_element_type=F32)


def backward_mine(flipped, weights_t, *refs):
    *pieces, out, slopes, back = refs
    out[...] = item_terms(0, flipped, weights_t, pieces, slopes, back).reshape(out.shape)


def backward_theirs(chips, few, flipped, weights_t, *refs):
    mine, theirs = refs[:chips], refs[chips:2 * chips]
    before, keep, got, *outs, their_slopes, back, items, turned, slopes, chunks = refs[2 * chips:]
    chip, core = here()
    user = lax.axis_index("user")
    levels = weights_t.shape[0]
    terms = item_terms(1, flipped, weights_t, theirs, their_slopes, back)
    items[...] = before[...] + terms.reshape(items.shape)

    share = mine[0].shape[0]
    kept, part, columns = keep.shape
    rows = columns // (2 * levels)
    for k in range(chips):
        for other, pieces in enumerate((mine, theirs)):
            row = ((core ^ other) * chips + (chip ^ k)) * share
            slopes[pl.ds(pl.multiple_of(row, share), share), :] = pieces[k][...]
    for k in range(kept):
        total = (keep[k] + got[k].astype(F32)).astype(BF16)
        for p in range(2):
            for r in range(levels):
                at, column = (k * levels + r) * part, (p * levels + r) * rows
                turned[at:at + part, p * rows:(p + 1) * rows] = total[:, column:column + rows]
    terms = jnp.dot(turned[...], slopes[...], preferred_element_type=F32)
    users = chunks.shape[0]
    groups = part // few
    for u in range(users):
        for block in range(kept * levels):
            first = block * part + (u % groups) * few
            column = (u // groups) * LANES
            chunks[u, block * few:(block + 1) * few] = terms[first:first + few, column:column + LANES]

    _, tile, width = items.shape
    item_few = tile // users
    for k, out in enumerate(outs):
        first = pl.multiple_of((user ^ k) * item_few, item_few)
        blocks = [
            items[z, pl.ds(first, item_few), column:column + LANES]
            for column in range(0, width, LANES)
            for z in range(chips)
        ]
        fill(out, *blocks, chunks[user ^ k])


def fill(out, *blocks):
    at = 0
    for block in blocks:
        out[at:at + block.shape[0]] = block.astype(out.dtype)
        at += block.shape[0]
    if at < out.shape[0]:
        out[at:] = jnp.zeros((out.shape[0] - at,) + out.shape[1:], out.dtype)


def user_sum(chips, few, blocks, rows, *refs):
    count = len(refs) - chips - 1
    parts, outs, total = refs[:count], refs[count:-1], refs[-1]
    chip, _ = here()
    summed = parts[0][...]
    for part in parts[1:]:
        summed = summed + part[...].astype(F32)
    for block in range(blocks):
        for z in range(chips):
            at = (block * chips + z) * few
            total[z, block * few:(block + 1) * few] = summed[at:at + few]
    first = blocks * chips * few
    weight = summed[first:first + rows].astype(BF16)
    for k, out in enumerate(outs):
        fill(out, total[chip ^ k], weight)


def line_sum(items, rows, stride, own, *refs):
    *parts, out = refs
    made = dict(zip(reach(len(parts)), parts))
    parts = [own] + [made[k] for k in sorted(made)]
    total = own[:items]
    for part in parts[1:]:
        total = total + part[:items].astype(F32)
    blocks = [total]
    for k in range(len(parts)):
        terms = []
        for j in range(k % stride, len(parts), stride):
            at = items + ((j ^ k) // stride) * rows
            terms.append(parts[j][at:at + rows].astype(BF16).astype(F32))
        blocks.append(tree_sum(terms))
    fill(out, *blocks)


def weight_out(chips, items, few, scale, counts, *refs):
    users, places = counts
    pieces = refs[:users + len(places)]
    out, wide, loose, item_rows, sems = refs[-5:]
    chip, core = here()
    user = lax.axis_index("user")
    _, levels, half, hidden = wide.shape
    part = half // chips
    groups = part // few
    copies = []

    def send(source, target):
        copies.append(pltpu.make_async_copy(source, target, sems.at[len(copies)]))
        copies[-1].start()

    def rows_of(piece, k, r):
        at = items + (k * levels + r) * few
        return piece[at:at + few].astype(F32) * scale

    if users:
        item_few = item_rows.shape[0] // users
        for j in range(users):
            row = pl.multiple_of((user ^ j) * item_few, item_few)
            for block in range(items // item_few):
                item_rows[pl.ds(row, item_few), block * LANES:(block + 1) * LANES] = (
                    pieces[j][block * item_few:(block + 1) * item_few].astype(F32)
                )
        send(item_rows, refs[-6])
    for other, js in ((0, range(users)), (1, places)):
        first = pl.multiple_of((core ^ other) * half, half)
        base = users if other else 0
        for r in range(levels):
            for at, j in enumerate(js):
                column = pl.multiple_of((user ^ j) // groups * LANES, LANES)
                for k in range(chips):
                    block = rows_of(pieces[base + at], k, r)
                    if groups == 1:
                        row = pl.multiple_of((chip ^ k) * part, part)
                        wide[other, r, pl.ds(row, part), pl.ds(column, LANES)] = block
                    else:
                        loose[chip ^ k, user ^ j] = block
                if groups == 1 and other:
                    send(wide.at[other, r, :, pl.ds(column, LANES)],
                         out.at[r, pl.ds(first, half), pl.ds(column, LANES)])
            if groups > 1 and len(js):
                for z in range(chips):
                    for u in range(len(js)):
                        row, column = z * part + (u % groups) * few, (u // groups) * LANES
                        wide[other, r, row:row + few, column:column + LANES] = loose[z, u]
            if len(js) and (groups > 1 or not other):
                send(wide.at[other, r], out.at[r, pl.ds(first, half), :])
    for copy in copies:
        copy.wait()


def per_device(item_features, level_weights, tile_values, tile_order, tile_counts, cotangent):
    item_size = lax.axis_size("item")
    user_size = lax.axis_size("user")
    chips = item_size // 2
    levels, width, hidden_width = level_weights.shape
    tile = tile_values.shape[-1]
    capacity = tile_values.shape[2]
    items = item_features.shape[0] * item_size
    block_count = items // tile
    user_blocks = tile_order.shape[1] // (levels * block_count)
    group_rows = user_blocks * tile
    share = group_rows // item_size
    rows = levels * chips * share
    vmem, anywhere = space(pltpu.VMEM), space(pl.ANY)

    strips = tile // (2 * share)
    tiles = tile_values.reshape(1, capacity, strips, 2, share, tile)
    other_tiles = swap(tiles, "item", 1)
    far = swap_each([item_features] * (chips - 1), "item", 2)
    dense = call(
        functools.partial(place_tiles, block_count),
        struct((2, rows, items), BF16),
        (hbm(tile_order), hbm(tile_counts), hbm(tiles), other_tiles),
        4,
        scratch=[
            pltpu.SMEM(tile_order.shape, jnp.int32),
            pltpu.SMEM(tile_counts.shape, jnp.int32),
            pltpu.SemaphoreType.DMA((2 * capacity * strips + 2,)),
        ],
        specs=[space(pltpu.HBM)] * 3 + [anywhere],
    )
    far, dense = together(far, dense)
    mine = [item_features, *far]
    theirs = [swap(piece, "item", 1) for piece in mine]
    half_features = struct((items // 2, width), BF16)
    my_features, aggregate = call(
        forward_mine,
        (half_features, struct((rows, width), F32)),
        (dense, *mine),
        0.7,
    )
    piece = struct((share, hidden_width), BF16)
    their_features, pre_own, *pre_sends = call(
        functools.partial(forward_theirs, chips),
        (half_features, struct((share, hidden_width), F32)) + (piece,) * (chips - 1),
        (dense, level_weights, *theirs, aggregate),
        1,
        scratch=[pltpu.VMEM((chips, share, hidden_width), F32)],
    )
    pre_parts = swap_each(pre_sends, "item", 2)

    part = width // item_size
    kept = chips // 2
    turned_own, turned_send = call(
        functools.partial(turn, levels),
        (struct((kept, part, 2 * rows), F32), struct((kept, part, 2 * rows), BF16)),
        (dense, my_features, their_features),
        3,
        scratch=[pltpu.VMEM((chips, part, 2 * rows), F32)],
    )
    turned_got = swap(turned_send, "item", 2)

    flipped, weights_t = call(
        flip,
        (struct((2, items // 2, rows), BF16), struct((levels, hidden_width, width), BF16)),
        (dense, level_weights),
        1.5,
    )
    *pre_parts, flipped, weights_t = lax.optimization_barrier(
        (*by_reach(pre_parts), flipped, weights_t)
    )
    pre, slope = call(
        slopes_of,
        (struct((share, hidden_width), F32), piece),
        (pre_own, *pre_parts, cotangent),
        0.1,
    )
    far = swap_each([slope] * (chips - 1), "item", 2)
    hidden = call(activate, piece, (pre,), 0.7)
    mine = [slope, *far]
    theirs = [swap(piece, "item", 1) for piece in mine]
    *theirs, turned_got = lax.optimization_barrier((*theirs, turned_got))

    item_part = call(
        backward_mine,
        struct((chips, tile, width), F32),
        (flipped, weights_t, *mine),
        1,
        scratch=[
            pltpu.VMEM((chips * share, hidden_width), BF16), pltpu.VMEM((rows, width), BF16)
        ],
    )

    def padded(amount):
        return -(-amount // 16) * 16

    few = part * min(hidden_width // LANES, user_size) // user_size
    item_few = tile // user_size
    blocks = width // LANES
    count = kept * levels * few
    amount = padded(blocks * chips * item_few + count)
    own, *sends = call(
        functools.partial(backward_theirs, chips, few),
        (struct((amount, LANES), F32),) + (struct((amount, LANES), BF16),) * (user_size - 1),
        (flipped, weights_t, *mine, *theirs, item_part, turned_own, turned_got),
        1.3,
        scratch=[
            pltpu.VMEM((chips * share, hidden_width), BF16),
            pltpu.VMEM((rows, width), BF16),
            pltpu.VMEM((chips, tile, width), F32),
            pltpu.VMEM((kept * levels * part, group_rows), BF16),
            pltpu.VMEM((group_rows, hidden_width), BF16),
            pltpu.VMEM((user_size, count, LANES), F32),
        ],
    )
    parts = swap_each(sends, "user", 1)
    parts, = together(parts)
    amount = padded(blocks * item_few + count)
    own, *sends = call(
        functools.partial(user_sum, chips, item_few, blocks, count),
        (struct((amount, LANES), F32),) + (struct((amount, LANES), BF16),) * (chips - 1),
        (own, *parts[::-1]),
        0.1,
        scratch=[pltpu.VMEM((chips, blocks * item_few, LANES), F32)],
    )
    parts = swap_each(sends, "item", 2)
    *parts, hidden = lax.optimization_barrier((*by_reach(parts), hidden))
    amount = padded(blocks * item_few + chips * levels * few)
    gathered = call(
        functools.partial(line_sum, blocks * item_few, levels * few, chips // kept),
        struct((amount, LANES), BF16),
        (own, *parts),
        0.1,
    )
    gathered = [gathered] + swap_each([gathered] * (user_size - 1), "user", 1)
    others = [swap(piece, "item", 1) for piece in gathered]
    weight_grad = struct((levels, width, hidden_width), F32)
    late = list(range(user_size))
    soon = [late.pop(0)] if few == part else []
    scratch = [
        pltpu.VMEM((2, levels, width // 2, hidden_width), F32),
        pltpu.VMEM((chips, user_size, few, LANES), F32),
        pltpu.VMEM((tile, width), F32),
        pltpu.SemaphoreType.DMA((levels * (user_size + 1) + 1,)),
    ]
    put = functools.partial(
        weight_out, chips, blocks * item_few, few, (group_rows * user_size) ** -0.5
    )
    item_grad, half_grad = call(
        functools.partial(put, (user_size, soon)),
        (struct((tile, width), F32), weight_grad),
        (*gathered, *[others[j] for j in soon]),
        0.9,
        scratch=scratch,
        out_specs=(anywhere, anywhere),
    )
    weight_grad = call(
        functools.partial(put, (0, late)),
        weight_grad,
        (*[others[j] for j in late], half_grad),
        0.9,
        scratch=scratch,
        specs=[vmem] * len(late) + [anywhere],
        out_specs=anywhere,
        aliases={len(late): 0},
    )
    return hidden, item_grad, weight_grad


def solution(mesh):
    in_specs = (
        P("item", None),
        P(),
        P("user", "item", None, None, None),
        P("user", None),
        P("user", None),
        P(("user", "item"), None),
    )
    out_specs = (P(("user", "item"), None), P("item", None), P())
    return jax.shard_map(
        per_device, mesh=mesh, in_specs=in_specs, out_specs=out_specs, check_vma=False
    )
```
